32 devices in a mesh: rows: 8 (over z, x), rank: 4 (over y, core).
Axes of the slice: x: 2, y: 2, z: 4, core: 2. Of those that a mesh axis runs over, the one named last changes fastest.
Arguments:
- tokens: bfloat16 [32768, 768], P(('rows', 'rank')), may hold values from -6 to 6
- w_query: bfloat16 [768, 768], P('rows'), may hold values from -0.21875 to 0.21875
- w_key: bfloat16 [768, 768], P('rows'), may hold values from -0.21875 to 0.21875
- w_value: bfloat16 [768, 768], P('rows'), may hold values from -0.21875 to 0.21875
- w_out: bfloat16 [768, 768], P('rows'), may hold values from -1.25 to 1.25
- w_up: bfloat16 [768, 3072], P('rows'), may hold values from -0.21875 to 0.21875
- w_down: bfloat16 [3072, 768], P('rows'), may hold values from -0.109375 to 0.109375
- gain_one: float32 [768], replicated, may hold values from 0.5 to 1.5
- shift_one: float32 [768], replicated, may hold values from -1.5 to 1.5
- gain_two: float32 [768], replicated, may hold values from 0.5 to 1.5
- shift_two: float32 [768], replicated, may hold values from -1.5 to 1.5
- adapter_a: bfloat16 [768, 1024], P(None, 'rank'), may hold values from -0.21875 to 0.21875
- adapter_b: bfloat16 [1024, 768], P('rank'), may hold values from -0.1875 to 0.1875
- query_rank_scale: bfloat16 [1024], P('rank'), may hold values from 0.29882812 to 1.5
- value_rank_scale: bfloat16 [1024], P('rank'), may hold values from 0.29882812 to 1.5
- query_out_scale: bfloat16 [768], replicated, may hold values from -4 to 4
- value_out_scale: bfloat16 [768], replicated, may hold values from -4 to 4
- segments: int32 [64, 512], P(('rows', 'rank')), may hold values from 0 to 15, never falling along the last dimension, each value on 1 to 128 neighbouring positions
- cotangent: bfloat16 [32768, 768], P(('rows', 'rank')), may hold values from -6 to 6
Outputs:
- layer_out: bfloat16 [32768, 768], P(('rows', 'rank'))
- input_grad: bfloat16 [32768, 768], P(('rows', 'rank'))
- grad_query_rank: float32 [1024], P('rank')
- grad_value_rank: float32 [1024], P('rank')
- grad_query_out: float32 [768], replicated
- grad_value_out: float32 [768], replicated
The draws below stay inside these ranges and needn't reach their ends.
Inputs may be any that keep to these rules, and one draw needn't show every extreme that they name: `segments`: segment numbers never fall along a packed row of 512 tokens; a token attends only to tokens of its own row and segment.
All inputs are finite; a program needn't handle non-finite values.
Results may differ from the reference program's by a relative error of at most 0.029.
Values may be sent and summed in bfloat16 or wider, within the bound.
A program may use at most 192 MiB of HBM per device.

```python
import math
import jax
import jax.numpy as jnp
import numpy as np
from jax import lax

D = 768
HEADS = 12
HEAD = 64
FF = 3072
RANK = 1024
SEQ = 512
SEG_COUNT = 16
SEG_MOST = 128
BATCH_ROWS = 64
TOKENS = 32768


def block_scale(key, extent, cuts, smallest, top_value):
    factor_of, own = 1.0, jax.random.fold_in(key, 6)
    for dim, blocks in cuts:
        steps = jnp.exp(jax.random.uniform(jax.random.fold_in(own, dim), (blocks,), jnp.float32, smallest / len(cuts), top_value / len(cuts)))
        factor_of = factor_of * jnp.repeat(steps, extent[dim] // blocks).reshape([-1 if axis == dim else 1 for axis in range(len(extent))])
    return factor_of


def split_up(number_of, total, most, slope):
    weights = [(1 << 20) // math.isqrt(rank ** slope) + 1 for rank in range(2, number_of + 1)]
    spare, counts = total - most - (number_of - 1), [1] * (number_of - 1)
    while spare > 0:
        free = [i for i in range(number_of - 1) if counts[i] < most]
        pool, left = sum([weights[i] for i in free]), spare
        for i in free:
            more = min(most - counts[i], max(1, left * weights[i] // pool), spare)
            counts[i] = counts[i] + more
            spare = spare - more
    return np.array([most] + counts)


def ragged_sizes(rng, count, total, reach, lean):
    if count == 2:
        one = jax.random.randint(rng, (), max(1, total - reach), min(reach, total - 1) + 1)
        return jnp.stack([one, total - one])
    sizes = jnp.asarray(split_up(count, total, reach, lean), jnp.int32)
    pairs = (count - 1) // 2
    donor, receiver = sizes[1:1 + 2 * pairs:2], sizes[2:2 + 2 * pairs:2]
    margin = jnp.minimum(donor - 1, reach - receiver)
    moved = jax.random.randint(jax.random.fold_in(rng, 1), (pairs,), 0, 1 << 20) % (margin + 1)
    sizes = sizes.at[1:1 + 2 * pairs:2].set(donor - moved).at[2:2 + 2 * pairs:2].set(receiver + moved)
    return sizes[jax.random.permutation(jax.random.fold_in(rng, 2), count)]


def gaussian(key, shape, width, limit, cuts=(), dtype=jnp.bfloat16):
    entries = jax.random.normal(key, shape, jnp.float32) * width
    if len(cuts) > 0:
        entries = block_scale(key, shape, cuts, -0.22, 0.18) * entries
    return jnp.clip(entries, min=-limit, max=limit).astype(dtype)


def setup_inputs(seed: int = 0) -> dict:
    seeds = jax.random.split(jax.random.key(seed), 20)
    tokens = gaussian(seeds[0], (TOKENS, D), 1.0, 6.0, ((0, 32),))
    w_query = gaussian(seeds[1], (D, D), D ** -0.5, 0.21875, ((0, 8),))
    w_key = gaussian(seeds[2], (D, D), D ** -0.5, 0.21875, ((0, 8),))
    w_value = gaussian(seeds[3], (D, D), D ** -0.5, 0.21875, ((0, 8),))
    w_out = gaussian(seeds[4], (D, D), (D // 32) ** -0.5, 1.25, ((0, 8),))
    w_up = gaussian(seeds[5], (D, FF), D ** -0.5, 0.21875, ((0, 8),))
    w_down = gaussian(seeds[6], (FF, D), FF ** -0.5, 0.109375, ((0, 8),))
    gain_one = jnp.clip(1.0 + 0.1 * jax.random.normal(seeds[7], (D,), jnp.float32), 0.5, 1.5)
    shift_one = gaussian(seeds[8], (D,), 0.3, 1.5, (), jnp.float32)
    gain_two = jnp.clip(1.0 + 0.1 * jax.random.normal(seeds[9], (D,), jnp.float32), 0.5, 1.5)
    shift_two = gaussian(seeds[10], (D,), 0.3, 1.5, (), jnp.float32)
    adapter_a = gaussian(seeds[11], (D, RANK), D ** -0.5, 0.21875, ((1, 4),))
    adapter_b = gaussian(seeds[12], (RANK, D), RANK ** -0.5, 0.1875, ((0, 4),))
    query_rank_scale = jnp.clip(jnp.exp(math.log(1.5) - 1.6133518 * jax.random.uniform(seeds[13], (RANK,), jnp.float32) ** block_scale(seeds[13], (RANK,), ((0, 4),), -0.2, 0.2)), 0.29882812, 1.5).astype(jnp.bfloat16)
    value_rank_scale = jnp.clip(jnp.exp(math.log(1.5) - 1.6133518 * jax.random.uniform(seeds[14], (RANK,), jnp.float32) ** block_scale(seeds[14], (RANK,), ((0, 4),), -0.2, 0.2)), 0.29882812, 1.5).astype(jnp.bfloat16)
    query_out_scale = gaussian(seeds[15], (D,), 1.0, 4.0)
    value_out_scale = gaussian(seeds[16], (D,), 1.0, 4.0)
    segments = jax.vmap(lambda own: jnp.searchsorted(jnp.cumsum(ragged_sizes(own, SEG_COUNT, SEQ, SEG_MOST, 2)), jnp.arange(SEQ), side="right"))(jax.random.split(seeds[17], BATCH_ROWS)).reshape((BATCH_ROWS, SEQ)).astype(jnp.int32)
    cotangent = gaussian(seeds[18], (TOKENS, D), 1.0, 6.0, ((0, 32),))
    return dict(tokens=tokens, w_query=w_query, w_key=w_key, w_value=w_value, w_out=w_out, w_up=w_up, w_down=w_down, gain_one=gain_one, shift_one=shift_one, gain_two=gain_two, shift_two=shift_two, adapter_a=adapter_a, adapter_b=adapter_b, query_rank_scale=query_rank_scale, value_rank_scale=value_rank_scale, query_out_scale=query_out_scale, value_out_scale=value_out_scale, segments=segments, cotangent=cotangent)


@jax.custom_vjp
def low(v):
    return lax.optimization_barrier(v.astype(jnp.bfloat16)).astype(jnp.float32)

@jax.custom_vjp
def low_back(v):
    return v

def low_keep(v):
    return (low(v), None)

def low_pass(kept, grad):
    return (grad,)

def back_keep(v):
    return (v, None)

def back_low(kept, grad):
    return (low(grad),)
low.defvjp(low_keep, low_pass)
low_back.defvjp(back_keep, back_low)
epsilon = 1e-05
masked_score = -1e+30

def matmul(operand, matrix):
    return jnp.dot(operand, matrix, precision=lax.Precision.HIGHEST, preferred_element_type=jnp.float32)

def layer_norm(stream, norm_gain, norm_shift):
    centered = stream - lax.optimization_barrier(jnp.mean(stream, axis=-1, keepdims=True))
    spread = lax.optimization_barrier(jnp.mean(centered * centered, axis=-1, keepdims=True))
    return centered * lax.rsqrt(spread + epsilon) * norm_gain + norm_shift

def row_attend(pieces):
    queries, key_rows, values, segment_ids = pieces
    query_heads = queries.reshape(SEQ, HEADS, HEAD)
    key_heads = key_rows.reshape(SEQ, HEADS, HEAD)
    value_heads = values.reshape(SEQ, HEADS, HEAD)
    scores = jnp.einsum('qhd,khd->hqk', query_heads, key_heads, precision=lax.Precision.HIGHEST)
    scores = low_back(scores / math.sqrt(HEAD))
    same_doc = segment_ids[:, None] == segment_ids[None, :]
    scores = jnp.where(same_doc[None], scores, masked_score)
    row_peak = lax.optimization_barrier(jnp.max(scores, axis=-1, keepdims=True))
    weights = jnp.exp(scores - row_peak)
    attention = weights / lax.optimization_barrier(jnp.sum(weights, axis=-1, keepdims=True))
    mixture = jnp.einsum('hqk,khd->qhd', low(attention), value_heads, precision=lax.Precision.HIGHEST)
    return mixture.reshape(SEQ, HEADS * HEAD)

def forward(tokens, query_rank, value_rank, query_out, value_out, frozen, segments):
    w_query, w_key, w_value, w_out, w_up, w_down, gain_one, shift_one, gain_two, shift_two, adapter_a, adapter_b = frozen
    hidden_rank = low_back(matmul(tokens, adapter_a))
    ranked_query = low(hidden_rank * query_rank)
    ranked_value = low(hidden_rank * value_rank)
    part_query = low_back(matmul(ranked_query, adapter_b))
    part_value = low_back(matmul(ranked_value, adapter_b))
    queries = low_back(low(matmul(tokens, w_query) + part_query * query_out))
    key_rows = low_back(low(matmul(tokens, w_key)))
    values = low_back(low(matmul(tokens, w_value) + part_value * value_out))
    mixture = lax.map(jax.checkpoint(row_attend), (queries.reshape(-1, SEQ, D), key_rows.reshape(-1, SEQ, D), values.reshape(-1, SEQ, D), segments))
    mixture = low_back(low(mixture.reshape(-1, D)))
    attn_branch = low_back(matmul(mixture, w_out))
    normed_one = layer_norm(tokens + attn_branch, gain_one, shift_one)
    up_proj = low_back(matmul(low(normed_one), w_up))
    activated = low(jax.nn.gelu(up_proj, approximate=False))
    ffn_branch = low_back(matmul(activated, w_down))
    return layer_norm(normed_one + ffn_branch, gain_two, shift_two)

def reference(tokens, w_query, w_key, w_value, w_out, w_up, w_down, gain_one, shift_one, gain_two, shift_two, adapter_a, adapter_b, query_rank_scale, value_rank_scale, query_out_scale, value_out_scale, segments, cotangent):
    frozen = tuple((item.astype(jnp.float32) for item in (w_query, w_key, w_value, w_out, w_up, w_down, gain_one, shift_one, gain_two, shift_two, adapter_a, adapter_b)))

    def closed(inputs, query_rank, value_rank, query_out, value_out):
        return forward(inputs, query_rank, value_rank, query_out, value_out, frozen, segments)
    layer_out, pullback = jax.vjp(closed, tokens.astype(jnp.float32), query_rank_scale.astype(jnp.float32), value_rank_scale.astype(jnp.float32), query_out_scale.astype(jnp.float32), value_out_scale.astype(jnp.float32))
    input_grad, grad_query_rank, grad_value_rank, grad_query_out, grad_value_out = pullback(cotangent.astype(jnp.float32))
    return (layer_out.astype(jnp.bfloat16), input_grad.astype(jnp.bfloat16), grad_query_rank, grad_value_rank, grad_query_out, grad_value_out)
```

```python
from functools import partial
import math

import jax
import jax.numpy as jnp
from jax import lax
from jax.experimental import pallas as pl
from jax.experimental.pallas import tpu as pltpu
from jax.sharding import PartitionSpec as P

HEADS = 12
HEAD = 64
MESH = pl.DeviceIdType.MESH
epsilon = 1e-05
masked_score = -1e30


def norm_forward(stream, norm_gain, norm_shift):
    centered = stream - jnp.mean(stream, axis=-1, keepdims=True)
    inverse = lax.rsqrt(jnp.mean(centered * centered, axis=-1, keepdims=True) + epsilon)
    normed = centered * inverse
    return (normed * norm_gain + norm_shift, normed, inverse)


def norm_backward(upstream, normed, inverse, norm_gain):
    scaled = upstream * norm_gain
    mean_grad = jnp.mean(scaled, axis=-1, keepdims=True)
    mean_cross = jnp.mean(scaled * normed, axis=-1, keepdims=True)
    return inverse * (scaled - mean_grad - normed * mean_cross)


def dot(a, b):
    return jnp.dot(a, b, preferred_element_type=jnp.float32)


def transpose_dot(operand, matrix):
    return lax.dot_general(
        operand, matrix, (((1,), (1,)), ((), ())), preferred_element_type=jnp.float32
    )


def head_scores(query_heads, key_heads, segment_ids):
    scores = jnp.einsum(
        "qhd,khd->hqk", query_heads, key_heads, preferred_element_type=jnp.float32
    ) / math.sqrt(HEAD)
    same_doc = segment_ids[:, None] == segment_ids[None, :]
    return jnp.where(same_doc[None], scores, masked_score)


def attend_forward(pieces):
    query_heads, key_heads, value_heads, segment_ids = pieces
    scores = head_scores(query_heads, key_heads, segment_ids)
    row_peak = jnp.max(scores, axis=-1, keepdims=True)
    weights = jnp.exp(scores - row_peak)
    row_total = jnp.sum(weights, axis=-1, keepdims=True)
    attention = weights / row_total
    mixture = jnp.einsum(
        "hqk,khd->qhd",
        attention.astype(jnp.bfloat16),
        value_heads,
        preferred_element_type=jnp.float32,
    )
    return (mixture, row_peak + jnp.log(row_total))


def attend_backward(pieces):
    query_heads, key_heads, value_heads, grad_heads, segment_ids, log_total = pieces
    scores = head_scores(query_heads, key_heads, segment_ids)
    attention = jnp.exp(scores - log_total)
    grad_attn = jnp.einsum(
        "qhd,khd->hqk", grad_heads, value_heads, preferred_element_type=jnp.float32
    )
    centre = jnp.sum(attention * grad_attn, axis=-1, keepdims=True)
    grad_scores = (attention * (grad_attn - centre)).astype(jnp.bfloat16)
    grad_query = (
        jnp.einsum("hqk,khd->qhd", grad_scores, key_heads, preferred_element_type=jnp.float32)
        / math.sqrt(HEAD)
    ).astype(jnp.bfloat16)
    grad_key = (
        jnp.einsum("hqk,qhd->khd", grad_scores, query_heads, preferred_element_type=jnp.float32)
        / math.sqrt(HEAD)
    ).astype(jnp.bfloat16)
    grad_value = jnp.einsum(
        "hqk,qhd->khd",
        attention.astype(jnp.bfloat16),
        grad_heads,
        preferred_element_type=jnp.float32,
    ).astype(jnp.bfloat16)
    return (grad_query, grad_key, grad_value)


def gather_kernel(pieces, shards, count, *refs):
    ins, outs = refs[:count], refs[count : 2 * count]
    local_sem, sz, rz, sx, rx, sy, ry, sp, rp, sq, rq = refs[2 * count :]
    row, rank = lax.axis_index("rows"), lax.axis_index("rank")
    z, x, y, c = row // 2, row % 2, rank // 2, rank % 2
    other_z = (z, z + 1 - 2 * (z % 2), (z + 2) % 4, 3 - z)
    to_z = [(other_z[d] * 2 + x, rank) for d in range(4)]
    to_x = (z * 2 + 1 - x, rank)
    to_y = (row, (1 - y) * 2 + c)
    to_core = (row, y * 2 + 1 - c)
    barrier = pltpu.get_barrier_semaphore()
    friends = to_z[1:] + [to_x, to_y, to_core]
    for friend in friends:
        pl.semaphore_signal(barrier, inc=1, device_id=friend, device_id_type=MESH)
    pl.semaphore_wait(barrier, len(friends))

    def rows_of(p, shard, offset, size):
        m, first, total, _ = pieces[p]
        return pl.ds(pl.multiple_of(shard * shards[m] + first + offset, 16), size)

    def plane(p, shard, core):
        unit = pieces[p][2] // 6
        return rows_of(p, shard, 3 * unit * core + unit * y, 2 * unit)

    def half(p, shard, side, core):
        unit = pieces[p][2] // 6
        return rows_of(p, shard, 3 * unit * core + 2 * unit * side, unit)

    def here(p, rows):
        return outs[pieces[p][0]].at[rows]

    def remote(src, dst, send, recv, device):
        return pltpu.make_async_remote_copy(
            src_ref=src, dst_ref=dst, send_sem=send, recv_sem=recv,
            device_id=device, device_id_type=MESH,
        )

    def same(p, rows, send, recv, device):
        return remote(here(p, rows), here(p, rows), send, recv, device)

    def own(p):
        return ins[pieces[p][0]].at[plane(p, 0, c)]

    def shard(j):
        return other_z[j + 1] * 2 + x if j < 3 else other_z[j - 3] * 2 + 1 - x

    def send_z(p, d):
        return remote(own(p), here(p, plane(p, row, c)), sz.at[p, d - 1], rz.at[p, d - 1], to_z[d])

    def recv_z(p, d):
        return same(p, plane(p, shard(d - 1), c), sz.at[p, d - 1], rz.at[p, d - 1], to_z[d])

    def send_x(p, d):
        if d == 0:
            return remote(own(p), here(p, plane(p, row, c)), sx.at[p, 0], rx.at[p, 0], to_x)
        return same(p, plane(p, shard(d - 1), c), sx.at[p, d], rx.at[p, d], to_x)

    def recv_x(p, d):
        return same(p, plane(p, shard(3 + d), c), sx.at[p, d], rx.at[p, d], to_x)

    def send_y(p, j):
        return same(p, half(p, shard(j), y, c), sy.at[p, j], ry.at[p, j], to_y)

    def recv_y(p, j):
        return same(p, half(p, shard(j), 1 - y, c), sy.at[p, j], ry.at[p, j], to_y)

    def send_p(p, j):
        return same(p, plane(p, shard(j), c), sp.at[p, j], rp.at[p, j], to_core)

    def recv_p(p, j):
        return same(p, plane(p, shard(j), 1 - c), sp.at[p, j], rp.at[p, j], to_core)

    def send_q(p, j):
        return same(p, half(p, shard(j), 1 - y, c), sq.at[p, j], rq.at[p, j], to_core)

    def recv_q(p, j):
        return same(p, half(p, shard(j), 1 - y, 1 - c), sq.at[p, j], rq.at[p, j], to_core)

    total = len(pieces)
    ahead = 2
    local = [
        pltpu.make_async_copy(
            ins[m], outs[m].at[pl.ds(pl.multiple_of(row * shards[m], 16), shards[m])], local_sem.at[m]
        )
        for m in range(count)
    ]
    for copy in local:
        copy.start()

    def launch(p):
        for d in (1, 2, 3):
            send_z(p, d).start()
        send_x(p, 0).start()

    for p in range(ahead):
        launch(p)
    for t in range(total + 2):
        if t < total:
            recv_x(t, 0).wait_recv()
            send_y(t, 3).start()
            send_p(t, 3).start()
            for d in (1, 2, 3):
                recv_z(t, d).wait_recv()
                send_x(t, d).start()
                send_y(t, d - 1).start()
                send_p(t, d - 1).start()
        if t + ahead < total:
            launch(t + ahead)
        if 0 <= t - 1 < total:
            for d in (1, 2, 3):
                recv_x(t - 1, d).wait_recv()
                send_y(t - 1, 3 + d).start()
                send_p(t - 1, 3 + d).start()
        if 0 <= t - 2 < total:
            for j in range(7):
                recv_y(t - 2, j).wait_recv()
                send_q(t - 2, j).start()
    for p in range(total):
        for j in range(7):
            recv_p(p, j).wait_recv()
            recv_q(p, j).wait_recv()
    for copy in local:
        copy.wait()
    for p in range(total):
        for d in (1, 2, 3):
            send_z(p, d).wait_send()
        for d in range(4):
            send_x(p, d).wait_send()
        for j in range(7):
            send_y(p, j).wait_send()
            send_p(p, j).wait_send()
            send_q(p, j).wait_send()


def gather_weights(mesh_shape, weights):
    if mesh_shape != (8, 4) or any(w.shape[0] % 96 for w in weights):
        return [lax.all_gather(w, "rows", axis=0, tiled=True) for w in weights]
    shards = [w.shape[0] for w in weights]
    pieces = []
    for m, w in enumerate(weights):
        parts = max(1, w.shape[0] // 192)
        for part in range(parts):
            pieces.append((m, part * (w.shape[0] // parts), w.shape[0] // parts, w.shape[1]))
    count, total = len(weights), len(pieces)
    sem = pltpu.SemaphoreType.DMA
    anywhere = pl.BlockSpec(memory_space=pl.ANY)
    return pl.pallas_call(
        partial(gather_kernel, pieces, shards, count),
        out_shape=[
            jax.ShapeDtypeStruct((w.shape[0] * mesh_shape[0], w.shape[1]), w.dtype) for w in weights
        ],
        in_specs=[anywhere] * count,
        out_specs=[anywhere] * count,
        scratch_shapes=[sem((count,))] + [sem((total, n)) for n in (3, 3, 4, 4, 7, 7, 7, 7, 7, 7)],
        compiler_params=pltpu.CompilerParams(collective_id=0, has_side_effects=True),
    )(*weights)


def per_device(
    mesh_shape,
    tokens,
    w_query,
    w_key,
    w_value,
    w_out,
    w_up,
    w_down,
    gain_one,
    shift_one,
    gain_two,
    shift_two,
    adapter_a,
    adapter_b,
    query_rank_scale,
    value_rank_scale,
    query_out_scale,
    value_out_scale,
    segments,
    cotangent,
):
    local_rows, width = tokens.shape
    rows_here, row_length = segments.shape
    rank_here = adapter_a.shape[1]

    def split_heads(tensor_rows):
        return tensor_rows.reshape(rows_here, row_length, HEADS, HEAD)

    full_a = lax.all_gather(adapter_a, "rank", axis=1, tiled=True)
    full_b = lax.all_gather(adapter_b, "rank", axis=0, tiled=True)
    scales = lax.all_gather(
        jnp.stack([query_rank_scale, value_rank_scale]), "rank", axis=1, tiled=True
    )
    full_key, full_query, full_value, full_out, full_up, full_down = gather_weights(
        mesh_shape, [w_key, w_query, w_value, w_out, w_up, w_down]
    )
    merged_query = (
        full_query + dot((full_a * scales[0]), full_b) * query_out_scale.astype(jnp.float32)
    ).astype(jnp.bfloat16)
    merged_value = (
        full_value + dot((full_a * scales[1]), full_b) * value_out_scale.astype(jnp.float32)
    ).astype(jnp.bfloat16)
    queries = dot(tokens, merged_query).astype(jnp.bfloat16)
    key_rows = dot(tokens, full_key).astype(jnp.bfloat16)
    values = dot(tokens, merged_value).astype(jnp.bfloat16)
    mixture, log_total = lax.map(
        attend_forward, (split_heads(queries), split_heads(key_rows), split_heads(values), segments)
    )
    mixture_low = mixture.reshape(local_rows, width).astype(jnp.bfloat16)
    first_sum = tokens.astype(jnp.float32) + dot(mixture_low, full_out)
    normed_out, normed_one, inverse_one = norm_forward(first_sum, gain_one, shift_one)
    up_proj = dot(normed_out.astype(jnp.bfloat16), full_up)
    activated = jax.nn.gelu(up_proj, approximate=False).astype(jnp.bfloat16)
    second_sum = normed_out + dot(activated, full_down)
    layer_out, normed_two, inverse_two = norm_forward(second_sum, gain_two, shift_two)
    grad_second = norm_backward(cotangent.astype(jnp.float32), normed_two, inverse_two, gain_two)
    grad_act = transpose_dot(grad_second.astype(jnp.bfloat16), full_down)
    gelu_grad = jax.vjp(partial(jax.nn.gelu, approximate=False), up_proj)[1](grad_act)[0]
    grad_normed = grad_second + transpose_dot(gelu_grad.astype(jnp.bfloat16), full_up)
    grad_first = norm_backward(grad_normed, normed_one, inverse_one, gain_one)
    grad_mixture = transpose_dot(grad_first.astype(jnp.bfloat16), full_out).astype(jnp.bfloat16)
    grad_query, grad_key, grad_value = lax.map(
        attend_backward,
        (
            split_heads(queries),
            split_heads(key_rows),
            split_heads(values),
            split_heads(grad_mixture),
            segments,
            log_total,
        ),
    )
    grad_query = grad_query.reshape(local_rows, width)
    grad_key = grad_key.reshape(local_rows, width)
    grad_value = grad_value.reshape(local_rows, width)

    def token_product(grad):
        return lax.dot_general(
            tokens, grad, (((0,), (0,)), ((), ())), preferred_element_type=jnp.float32
        ).astype(jnp.bfloat16)

    def through_a(grad):
        return lax.dot_general(
            full_a, token_product(grad), (((0,), (0,)), ((), ())), preferred_element_type=jnp.float32
        )

    with_b_query = through_a(grad_query) * full_b.astype(jnp.float32)
    with_b_value = through_a(grad_value) * full_b.astype(jnp.float32)
    small = jnp.concatenate(
        [
            jnp.sum(with_b_query * query_out_scale.astype(jnp.float32), axis=1),
            jnp.sum(with_b_value * value_out_scale.astype(jnp.float32), axis=1),
            jnp.sum(with_b_query * scales[0].astype(jnp.float32)[:, None], axis=0),
            jnp.sum(with_b_value * scales[1].astype(jnp.float32)[:, None], axis=0),
        ]
    )
    small = lax.psum(small, ("rows", "rank"))
    all_ranks = full_b.shape[0]
    mine = lax.axis_index("rank") * rank_here
    input_sum = (
        grad_first
        + transpose_dot(grad_query, merged_query)
        + transpose_dot(grad_key, full_key)
        + transpose_dot(grad_value, merged_value)
    )
    return (
        layer_out.astype(jnp.bfloat16),
        input_sum.astype(jnp.bfloat16),
        lax.dynamic_slice(small, (mine,), (rank_here,)),
        lax.dynamic_slice(small, (all_ranks + mine,), (rank_here,)),
        small[2 * all_ranks : 2 * all_ranks + width],
        small[2 * all_ranks + width :],
    )


def solution(mesh):
    return jax.shard_map(
        partial(per_device, (mesh.shape["rows"], mesh.shape["rank"])),
        mesh=mesh,
        in_specs=(
            P(("rows", "rank"), None),
            P("rows", None),
            P("rows", None),
            P("rows", None),
            P("rows", None),
            P("rows", None),
            P("rows", None),
            P(),
            P(),
            P(),
            P(),
            P(None, "rank"),
            P("rank", None),
            P("rank"),
            P("rank"),
            P(),
            P(),
            P(("rows", "rank"), None),
            P(("rows", "rank"), None),
        ),
        out_specs=(
            P(("rows", "rank"), None),
            P(("rows", "rank"), None),
            P("rank"),
            P("rank"),
            P(),
            P(),
        ),
        check_vma=False,
    )
```

```python
from functools import partial

import jax
import jax.numpy as jnp
from jax import lax
from jax.experimental import pallas as pl
from jax.experimental.pallas import tpu as pltpu
from jax.sharding import PartitionSpec as P

HEADS = 12
HEAD = 64
MESH = pl.DeviceIdType.MESH
epsilon = 1e-05
masked_score = -1e30
f32 = jnp.float32
bf16 = jnp.bfloat16
WINDOWS = ((0, 256), (0, 384), (128, 384), (256, 256))
AHEAD = 2
VMEM_LIMIT = 64 * 2**20


def dot(a, b):
    return jnp.dot(a, b, preferred_element_type=f32)


def dot_nt(a, b):
    return lax.dot_general(a, b, (((1,), (1,)), ((), ())), preferred_element_type=f32)


def dot_tn(a, b):
    return lax.dot_general(a, b, (((0,), (0,)), ((), ())), preferred_element_type=f32)


def flat(block):
    return block.reshape(block.shape[0] * block.shape[1] * block.shape[2], block.shape[3])


def mean(block):
    return jnp.mean(block, axis=1, keepdims=True)


def normalize(stream):
    centered = stream - mean(stream)
    inverse = lax.rsqrt(mean(centered * centered) + epsilon)
    return centered * inverse, inverse


def norm_backward(scaled, normed, inverse):
    return inverse * (scaled - mean(scaled) - normed * mean(scaled * normed))


def low_lanes():
    return lax.broadcasted_iota(jnp.int32, (128, 128), 1) < HEAD


def two_heads(block, low):
    zero = jnp.zeros_like(block)
    return jnp.concatenate([jnp.where(low, block, zero), jnp.where(low, zero, block)], axis=0)


class Links:
    def __init__(self, pieces, merged, ins, bufs, sems):
        self.pieces, self.merged, self.ins, self.bufs = pieces, merged, ins, bufs
        self.sems = sems
        self.row, self.rank = lax.axis_index("rows"), lax.axis_index("rank")
        self.z, self.x = self.row // 2, self.row % 2
        self.y, self.c = self.rank // 2, self.rank % 2
        z = self.z
        self.other = (z, z + 1 - 2 * (z % 2), (z + 2) % 4, 3 - z)
        self.middle = (z == 1) | (z == 2)
        self.to_z = [(self.other[d] * 2 + self.x, self.rank) for d in range(4)]
        self.to_x = (z * 2 + 1 - self.x, self.rank)
        self.to_y = (self.row, (1 - self.y) * 2 + self.c)
        self.to_core = (self.row, self.y * 2 + 1 - self.c)
        self.to_cross = (self.row, (1 - self.y) * 2 + 1 - self.c)
        self.rank_friends = [self.to_core, self.to_y, self.to_cross]
        self.row_friends = [
            (self.other[n // 2] * 2 + (self.x if n % 2 == 0 else 1 - self.x), self.rank)
            for n in range(1, 8)
        ]

    def enter(self):
        barrier = pltpu.get_barrier_semaphore()
        friends = self.rank_friends + self.row_friends
        for friend in friends:
            pl.semaphore_signal(barrier, inc=1, device_id=friend, device_id_type=MESH)
        pl.semaphore_wait(barrier, len(friends))

    def copy(self, src, dst, send, recv, device):
        return pltpu.make_async_remote_copy(
            src_ref=src, dst_ref=dst, send_sem=send, recv_sem=recv,
            device_id=device, device_id_type=MESH,
        )

    def same(self, ref, send, recv, device):
        return self.copy(ref, ref, send, recv, device)

    def unit(self, p):
        return self.pieces[p][1] // 6

    def cols(self, p):
        return pl.ds(self.pieces[p][2], self.pieces[p][3])

    def plane_rows(self, p):
        u = self.unit(p)
        return pl.ds(pl.multiple_of(3 * u * self.c + u * self.y, 16), 2 * u)

    def side_rows(self, p, side):
        u = self.unit(p)
        return pl.ds(pl.multiple_of(3 * u * self.c + 2 * u * side, 16), u)

    def core_rows(self, p, core):
        u = self.unit(p)
        return pl.ds(pl.multiple_of(3 * u * core, 16), 3 * u)

    def buf(self, p):
        return self.bufs[self.pieces[p][0]]

    def is_merged(self, p):
        return self.pieces[p][0] in self.merged

    def at(self, p, z):
        return self.buf(p).at[z, self.x, self.plane_rows(p), self.cols(p)]

    def own(self, p):
        if self.is_merged(p):
            return self.at(p, self.z)
        return self.ins[self.pieces[p][0]].at[self.plane_rows(p), self.cols(p)]

    def local(self, p):
        return pltpu.make_async_copy(
            self.ins[self.pieces[p][0]].at[self.core_rows(p, self.c), self.cols(p)],
            self.buf(p).at[self.z, self.x, self.core_rows(p, self.c), self.cols(p)],
            self.sems["local"].at[p],
        )

    def z_send(self, p, d):
        return self.copy(
            self.own(p), self.at(p, self.z), self.sems["sz"].at[p, d - 1], self.sems["rz"].at[p, d - 1],
            self.to_z[d],
        )

    def z_pass(self, p):
        return self.same(
            self.at(p, self.other[2]), self.sems["sz"].at[p, 3], self.sems["rz"].at[p, 2], self.to_z[1]
        )

    def z_recv(self, p, d):
        return self.same(
            self.at(p, self.other[d]), self.sems["sz"].at[p, d - 1], self.sems["rz"].at[p, d - 1],
            self.to_z[d],
        )

    def x_slice(self, p, x):
        return self.buf(p).at[:, x, self.plane_rows(p), self.cols(p)]

    def x_send(self, p):
        return self.same(self.x_slice(p, self.x), self.sems["sx"].at[p], self.sems["rx"].at[p], self.to_x)

    def x_recv(self, p):
        return self.same(
            self.x_slice(p, 1 - self.x), self.sems["sx"].at[p], self.sems["rx"].at[p], self.to_x
        )

    def y_one(self, p, d, side):
        ref = self.buf(p).at[self.other[d], self.x, self.side_rows(p, side), self.cols(p)]
        return self.same(ref, self.sems["sy"].at[p, d], self.sems["ry"].at[p, d], self.to_y)

    def y_many(self, p, side):
        ref = self.buf(p).at[:, 1 - self.x, self.side_rows(p, side), self.cols(p)]
        return self.same(ref, self.sems["sy"].at[p, 4], self.sems["ry"].at[p, 4], self.to_y)

    def core_copy(self, p, core):
        ref = self.buf(p).at[:, :, self.core_rows(p, core), self.cols(p)]
        return self.same(ref, self.sems["sk"].at[p], self.sems["rk"].at[p], self.to_core)

    def launch(self, p):
        if not self.is_merged(p):
            self.local(p).start()
        self.z_send(p, 2).start()
        self.z_send(p, 1).start()
        pl.when(self.middle)(lambda: self.z_send(p, 3).start())

    def stage_z(self, p):
        if self.is_merged(p):
            self.y_one(p, 0, self.y).start()
        else:
            self.local(p).wait()
        self.z_recv(p, 2).wait_recv()
        pl.when(self.middle)(lambda: self.z_pass(p).start())
        self.y_one(p, 2, self.y).start()
        for d in (1, 3):
            self.z_recv(p, d).wait_recv()
            self.y_one(p, d, self.y).start()
        self.x_send(p).start()

    def stage_x(self, p):
        self.x_recv(p).wait_recv()
        self.y_many(p, self.y).start()

    def stage_y(self, p):
        if self.is_merged(p):
            self.y_one(p, 0, 1 - self.y).wait_recv()
        for d in (1, 2, 3):
            self.y_one(p, d, 1 - self.y).wait_recv()
        self.y_many(p, 1 - self.y).wait_recv()
        self.core_copy(p, self.c).start()

    def tick(self, t):
        total = len(self.pieces)
        if t < total:
            self.stage_z(t)
        if t + AHEAD < total:
            self.launch(t + AHEAD)
        if 0 <= t - 1 < total:
            self.stage_x(t - 1)
        if 0 <= t - 2 < total:
            self.stage_y(t - 2)
        if 0 <= t - 3 < total:
            self.core_copy(t - 3, 1 - self.c).wait_recv()

    def drain(self):
        for p in range(len(self.pieces)):
            self.z_send(p, 1).wait_send()
            self.z_send(p, 2).wait_send()

            def inner():
                self.z_send(p, 3).wait_send()
                self.z_pass(p).wait_send()

            pl.when(self.middle)(inner)
            self.x_send(p).wait_send()
            if self.is_merged(p):
                self.y_one(p, 0, self.y).wait_send()
            for d in (1, 2, 3):
                self.y_one(p, d, self.y).wait_send()
            self.y_many(p, self.y).wait_send()
            self.core_copy(p, self.c).wait_send()


def layer_kernel(remote, pieces, names, *refs):
    r = dict(zip(names, refs))
    tok, cot, mix, hb, acc = r["tok"], r["cot"], r["mix"], r["hb"], r["acc"]
    q, k, v, dg, ac = r["q"], r["k"], r["v"], r["dg"], r["ac"]
    vecs, fa, fb, fs = r["vecs"], r["fa"], r["fb"], r["fs"]
    weights = [r[name] for name in ("wk", "wo", "wq", "wv", "wu", "wd")]
    wk, wo, wq, wv, wu, wd = weights
    ins = [r[name + "_in"] for name in ("wk", "wo", "wq", "wv", "wu", "wd")]
    width = tok.shape[1]
    rows = tok.shape[0]
    hidden = ac.shape[1]
    halves = [pl.ds(n * (rows // 2), rows // 2) for n in range(2)]
    chunks = [pl.ds(n * width, width) for n in range(hidden // width)]
    gain_one, shift_one, gain_two, shift_two = [vecs[n : n + 1, :] for n in range(4)]

    def load(src, dst, n):
        return pltpu.make_async_copy(src, dst, r["load"].at[n])

    load_tok, load_cot = load(r["tok_in"], tok, 0), load(r["cot_in"], cot, 1)
    load_tok.start()
    load_cot.start()
    if remote:
        links = Links(pieces, (2, 3), ins, weights, r)
        row, rank = links.row, links.rank
        mine = pl.ds(pl.multiple_of(rank * 256, 256), 256)
        adapter = [
            load(r["fa_in"], fa.at[:, mine], 2),
            load(r["fb_in"], fb.at[mine, :], 3),
            load(r["fs_in"], fs.at[:, mine], 4),
            load(r["fa_in"].at[pl.ds(pl.multiple_of(row * 96, 96), 96), :], r["a_rows"], 5),
            load(ins[2].at[links.plane_rows(2), :], r["own_qv"].at[0], 6),
            load(ins[3].at[links.plane_rows(3), :], r["own_qv"].at[1], 7),
        ]
        for copy in adapter:
            copy.start()
        links.enter()
        for p in range(AHEAD):
            links.launch(p)
    else:
        adapter = [load(r[n + "_in"], r[n], 2 + i) for i, n in enumerate(("fa", "fb", "fs"))]
        adapter += [load(src, dst, 5 + i) for i, (src, dst) in enumerate(zip(ins, weights))]
        for copy in adapter:
            copy.start()
    for copy in adapter:
        copy.wait()

    if remote:
        part, met = r["part"], r["met"]
        b_rows = fb[mine, :]
        for n in range(2):
            scaled = r["a_rows"][...].astype(f32) * r["fs_in"][n : n + 1, :].astype(f32)
            part[n] = dot(scaled.astype(bf16), b_rows).astype(bf16)

        def part_rows(y, c):
            return pl.ds(pl.multiple_of(48 * c + 16 * y, 16), 32)

        places = (
            (links.y, 1 - links.c), (1 - links.y, links.c), (1 - links.y, 1 - links.c)
        )
        parts = [
            links.copy(
                part.at[:, part_rows(*place), :], met.at[n], r["sm"].at[n], r["rm"].at[n],
                links.rank_friends[n],
            )
            for n, place in enumerate(places)
        ]
        for copy in parts:
            copy.start()
        for copy in parts:
            copy.wait_recv()
        for n, buf in enumerate((wq, wv)):
            total = part[n, part_rows(links.y, links.c), :].astype(f32)
            for slot in range(3):
                total = total + met[slot, n].astype(f32)
            joined = r["own_qv"][n].astype(f32) + total * vecs[4 + n : 5 + n, :]
            buf[links.z, links.x, links.plane_rows(2 + n), :] = joined.astype(bf16)

    bias, probs = [r["bias%d" % t] for t in range(4)], [r["probs%d" % t] for t in range(4)]
    segs = r["segs"][...].astype(f32)
    padded = jnp.concatenate([segs, jnp.zeros((14, segs.shape[1]), f32)], axis=0).astype(bf16)
    for b in range(2):
        pick = (lax.broadcasted_iota(jnp.int32, (16, 128), 0) == b).astype(f32).astype(bf16)
        column = dot_tn(padded, pick)
        for t, (start, size) in enumerate(WINDOWS):
            same = column[start : start + size, :] == segs[b : b + 1, 128 * t : 128 * t + 128]
            bias[t][b] = jnp.where(same, 0.0, masked_score)
    low = low_lanes()
    load_tok.wait()

    def project(weight, out, scale):
        out[...] = (dot(tok[...], flat(weight[...])) * scale).astype(bf16)

    def attend(b):
        for p in range(HEADS // 2):
            lanes = pl.ds(128 * p, 128)
            for t, (start, size) in enumerate(WINDOWS):
                here = pl.ds(pl.multiple_of(b * 512 + 128 * t, 128), 128)
                window = pl.ds(pl.multiple_of(b * 512 + start, 128), size)
                scores = dot_nt(k[window, lanes], two_heads(q[here, lanes], low))
                mask = bias[t][b]
                scores = jnp.where(jnp.concatenate([mask, mask], axis=1) < 0.0, masked_score, scores)
                weight = jnp.exp(scores - jnp.max(scores, axis=0, keepdims=True))
                weight = weight * (1.0 / jnp.sum(weight, axis=0, keepdims=True))
                attention = weight.astype(bf16)
                probs[t][b * (HEADS // 2) + p] = attention
                both = dot_tn(attention, v[window, lanes])
                mix[here, lanes] = jnp.where(low, both[:128], both[128:]).astype(bf16)

    def first_norm():
        for half in halves:
            stream = tok[half, :].astype(f32) + dot(mix[half, :], flat(wo[...]))
            normed, inverse = normalize(stream)
            r["n1"][half, :] = normed.astype(bf16)
            r["i1"][half, :] = inverse
            out = normed * gain_one + shift_one
            acc[half, :] = out
            hb[half, :] = out.astype(bf16)

    def up(n):
        proj = dot(hb[...], flat(wu[:, :, :, chunks[n]]))
        bell = jnp.exp(proj * proj * -0.5)
        area = 0.5 + 0.5 * lax.erf(proj * 0.7071067811865476)
        ac[:, chunks[n]] = (proj * area).astype(bf16)
        dg[:, chunks[n]] = (area + proj * bell * 0.3989422804014327).astype(bf16)

    third = pl.ds(0, width // 3), pl.ds(width // 3, width // 3), pl.ds(2 * (width // 3), width // 3)

    def down(n):
        acc[:, third[n]] = acc[:, third[n]] + dot(ac[...], flat(wd[:, :, :, third[n]]))

    send_out = [
        pltpu.make_async_copy(r["lo"].at[half, :], r["out"].at[half, :], r["store"].at[n])
        for n, half in enumerate(halves)
    ]

    def second_norm():
        for n, half in enumerate(halves):
            normed, inverse = normalize(acc[half, :])
            r["lo"][half, :] = (normed * gain_two + shift_two).astype(bf16)
            send_out[n].start()
            grad = norm_backward(cot[half, :].astype(f32) * gain_two, normed, inverse)
            acc[half, :] = grad
            hb[half, :] = grad.astype(bf16)

    steps = {
        3: [lambda: project(wk, k, 1.0)],
        5: [lambda: project(wq, q, 0.125)],
        6: [lambda: project(wv, v, 1.0), lambda: attend(0)],
        7: [lambda: attend(1)],
        8: [first_norm],
        9: [lambda: up(0)],
        10: [lambda: up(1)],
        11: [lambda: up(2), lambda: up(3)],
        12: [lambda: down(0)],
        13: [lambda: down(1), lambda: down(2)],
    }
    if remote:
        own_adapter = (fa.at[:, mine], fb.at[mine, :], fs.at[:, mine])
        theirs = pl.ds(pl.multiple_of(((1 - links.y) * 2 + links.c) * 256, 256), 256)
        got_adapter = (fa.at[:, theirs], fb.at[theirs, :], fs.at[:, theirs])
        core = pl.ds(pl.multiple_of((links.y * 2 + 1 - links.c) * 256, 256), 256)
        core_adapter = (fa.at[:, core], fb.at[core, :], fs.at[:, core])
        cross = pl.ds(pl.multiple_of(((1 - links.y) * 2 + 1 - links.c) * 256, 256), 256)
        cross_adapter = (fa.at[:, cross], fb.at[cross, :], fs.at[:, cross])

        def adapters(refs_, n, device):
            return [links.same(ref, r["sa"].at[n, i], r["ra"].at[n, i], device) for i, ref in enumerate(refs_)]

        for t in range(len(pieces) + 3):
            links.tick(t)
            if t == len(pieces):
                for copy in adapters(own_adapter, 0, links.to_y) + adapters(own_adapter, 1, links.to_core):
                    copy.start()
            for step in steps.get(t, ()):
                step()
    else:
        for t in sorted(steps):
            for step in steps[t]:
                step()
    load_cot.wait()
    second_norm()
    if remote:
        links.drain()
        for copy in parts:
            copy.wait_send()

    for n in range(hidden // width):
        grad = dot_nt(hb[...], wd[n].reshape(width, width))
        ac[:, chunks[n]] = (grad * dg[:, chunks[n]].astype(f32)).astype(bf16)
    if remote:
        for copy in adapters(got_adapter, 0, links.to_y):
            copy.wait_recv()
        passing = adapters(got_adapter, 2, links.to_core)
        for copy in passing:
            copy.start()
    for half in halves:
        grad = acc[half, :] + dot_nt(ac[half, :], flat(wu[...]))
        grad = norm_backward(grad * gain_one, r["n1"][half, :].astype(f32), r["i1"][half, :])
        acc[half, :] = grad
        hb[half, :] = grad.astype(bf16)
    heads = lax.broadcasted_iota(jnp.int32, (16, width), 1) // HEAD
    pick = (heads == lax.broadcasted_iota(jnp.int32, (16, width), 0)).astype(f32).astype(bf16)
    grad = dot_nt(hb[...], flat(wo[...]))
    dg[:, chunks[0]] = grad.astype(bf16)
    r["delta"][...] = dot_nt(pick, (grad * mix[...].astype(f32)).astype(bf16))
    delta = r["delta"]

    def attend_back(b, _):
        for p in range(HEADS // 2):
            lanes = pl.ds(128 * p, 128)
            keys, vals = [None] * 4, [None] * 4
            for t, (start, size) in enumerate(WINDOWS):
                here = pl.ds(pl.multiple_of(b * 512 + 128 * t, 128), 128)
                window = pl.ds(pl.multiple_of(b * 512 + start, 128), size)
                grad_pair = two_heads(dg[here, lanes], low)
                grad_attn = dot_nt(v[window, lanes], grad_pair)
                attention = probs[t][b * (HEADS // 2) + p]
                centre = jnp.concatenate(
                    [delta[2 * p : 2 * p + 1, here], delta[2 * p + 1 : 2 * p + 2, here]], axis=1
                )
                grad_scores = (attention.astype(f32) * (grad_attn - centre)).astype(bf16)
                both = dot_tn(grad_scores, k[window, lanes])
                both = jnp.where(low, both[:128], both[128:]) * 0.125
                dg[here, pl.ds(width + 128 * p, 128)] = both.astype(bf16)
                key_part = dot(grad_scores, two_heads(q[here, lanes], low))
                val_part = dot(attention, grad_pair)
                for total, piece in ((keys, key_part), (vals, val_part)):
                    for n in range(size // 128):
                        at = start // 128 + n
                        add = piece[128 * n : 128 * n + 128]
                        total[at] = add if total[at] is None else total[at] + add
            for t in range(4):
                here = pl.ds(pl.multiple_of(b * 512 + 128 * t, 128), 128)
                dg[here, pl.ds(2 * width + 128 * p, 128)] = keys[t].astype(bf16)
                dg[here, pl.ds(3 * width + 128 * p, 128)] = vals[t].astype(bf16)
        return 0

    lax.fori_loop(0, 2, attend_back, 0)

    square = pl.ds(0, width)
    ac[square, chunks[0]] = dot_tn(tok[...], dg[:, chunks[1]]).astype(bf16)
    ac[square, chunks[1]] = dot_tn(tok[...], dg[:, chunks[3]]).astype(bf16)
    if remote:
        for refs_, n in ((core_adapter, 1), (cross_adapter, 2)):
            for copy in adapters(refs_, n, links.to_core):
                copy.wait_recv()
    for n in range(2):
        ac[:, chunks[2 + n]] = (dot_tn(fa[...], ac[square, chunks[n]]) * fb[...].astype(f32)).astype(bf16)
    out_scales = jnp.concatenate([vecs[4:6, :], jnp.zeros((14, width), f32)], axis=0).astype(bf16)
    red = r["red"]
    red[28:32, :] = jnp.zeros((4, 128), f32)
    for n in range(2):
        along_rank = dot_nt(out_scales, ac[:, chunks[2 + n]])
        along_width = dot(fs[...], ac[:, chunks[2 + n]])
        for i in range(8):
            red[8 * n + i : 8 * n + i + 1, :] = along_rank[n : n + 1, 128 * i : 128 * i + 128]
        for i in range(6):
            at = 16 + 6 * n + i
            red[at : at + 1, :] = along_width[n : n + 1, 128 * i : 128 * i + 128]
    if remote:
        one, two = r["one"], r["two"]
        one[rank] = red[...]
        first = [
            links.copy(red, one.at[rank], r["s1"].at[n], r["r1"].at[n], friend)
            for n, friend in enumerate(links.rank_friends)
        ]
        for copy in first:
            copy.start()
    acc[...] = acc[...] + dot_nt(dg[:, chunks[2]], flat(wk[...]))
    if remote:
        for copy in first:
            copy.wait_recv()
        r["sum"][...] = (one[0] + one[1]) + (one[2] + one[3])
        two[row] = r["sum"][...]
        second = [
            links.copy(r["sum"], two.at[row], r["s2"].at[n], r["r2"].at[n], friend)
            for n, friend in enumerate(links.row_friends)
        ]
        for copy in second:
            copy.start()
    send_grad = [
        pltpu.make_async_copy(cot.at[half, :], r["grad"].at[half, :], r["store"].at[2 + n])
        for n, half in enumerate(halves)
    ]
    for n, half in enumerate(halves):
        grad = acc[half, :] + dot_nt(dg[half, chunks[1]], flat(wq[...]))
        grad = grad + dot_nt(dg[half, chunks[3]], flat(wv[...]))
        cot[half, :] = grad.astype(bf16)
        send_grad[n].start()
    if remote:
        for copy in second:
            copy.wait_recv()
        total = two[0]
        for n in range(1, 8):
            total = total + two[n]
        r["small"][...] = total
        for copy in first + second + passing:
            copy.wait_send()
        for copy in adapters(own_adapter, 0, links.to_y) + adapters(own_adapter, 1, links.to_core):
            copy.wait_send()
    else:
        r["small"][...] = red[...]
    for copy in send_out + send_grad:
        copy.wait()


def run_layer(remote, tokens, cotangent, weights, adapter_a, adapter_b, scales, vecs, segments):
    rows, width = tokens.shape
    hidden = weights[4].shape[-1]
    ranks = 1024
    sem = pltpu.SemaphoreType.DMA
    pieces = [(m, 96, 0, width) for m in range(4)]
    pieces += [(4, 96, n * width, width) for n in range(hidden // width)]
    pieces += [(5, 384, n * (width // 3), width // 3) for n in range(3)]
    total = len(pieces)
    block = (4, 2, width // 8, width)
    scratch = {
        "tok": pltpu.VMEM((rows, width), bf16),
        "cot": pltpu.VMEM((rows, width), bf16),
        "wk": pltpu.VMEM(block, bf16),
        "wo": pltpu.VMEM(block, bf16),
        "wq": pltpu.VMEM(block, bf16),
        "wv": pltpu.VMEM(block, bf16),
        "wu": pltpu.VMEM((4, 2, width // 8, hidden), bf16),
        "wd": pltpu.VMEM((4, 2, hidden // 8, width), bf16),
        "fa": pltpu.VMEM((width, ranks), bf16),
        "fb": pltpu.VMEM((ranks, width), bf16),
        "fs": pltpu.VMEM((16, ranks), bf16),
        "q": pltpu.VMEM((rows, width), bf16),
        "k": pltpu.VMEM((rows, width), bf16),
        "v": pltpu.VMEM((rows, width), bf16),
        "mix": pltpu.VMEM((rows, width), bf16),
        "n1": pltpu.VMEM((rows, width), bf16),
        "i1": pltpu.VMEM((rows, 1), f32),
        "hb": pltpu.VMEM((rows, width), bf16),
        "lo": pltpu.VMEM((rows, width), bf16),
        "dg": pltpu.VMEM((rows, hidden), bf16),
        "ac": pltpu.VMEM((rows, hidden), bf16),
        "acc": pltpu.VMEM((rows, width), f32),
        "delta": pltpu.VMEM((16, rows), f32),
        "red": pltpu.VMEM((32, 128), f32),
        "load": sem((16,)),
        "store": sem((4,)),
    }
    for t, (_, size) in enumerate(WINDOWS):
        scratch["bias%d" % t] = pltpu.VMEM((2, size, 128), f32)
        scratch["probs%d" % t] = pltpu.VMEM((HEADS, size, 256), bf16)
    if remote:
        scratch.update({
            "a_rows": pltpu.VMEM((96, 256), bf16),
            "own_qv": pltpu.VMEM((2, 32, width), bf16),
            "part": pltpu.VMEM((2, 96, width), bf16),
            "met": pltpu.VMEM((3, 2, 32, width), bf16),
            "one": pltpu.VMEM((4, 32, 128), f32),
            "two": pltpu.VMEM((8, 32, 128), f32),
            "sum": pltpu.VMEM((32, 128), f32),
            "local": sem((total,)),
            "sz": sem((total, 4)),
            "rz": sem((total, 3)),
            "sx": sem((total,)),
            "rx": sem((total,)),
            "sy": sem((total, 5)),
            "ry": sem((total, 5)),
            "sk": sem((total,)),
            "rk": sem((total,)),
            "sm": sem((3,)),
            "rm": sem((3,)),
            "sa": sem((3, 3)),
            "ra": sem((3, 3)),
            "s1": sem((3,)),
            "r1": sem((3,)),
            "s2": sem((7,)),
            "r2": sem((7,)),
        })
    order = ["tok_in", "cot_in", "wk_in", "wo_in", "wq_in", "wv_in", "wu_in", "wd_in", "fa_in", "fb_in"]
    names = order + ["fs_in", "vecs", "segs", "out", "grad", "small"] + list(scratch)
    anywhere, vmem = pl.BlockSpec(memory_space=pl.ANY), pl.BlockSpec(memory_space=pltpu.VMEM)
    params = dict(vmem_limit_bytes=VMEM_LIMIT, has_side_effects=True)
    if remote:
        params["collective_id"] = 0
    return pl.pallas_call(
        partial(layer_kernel, remote, pieces, names),
        out_shape=[
            jax.ShapeDtypeStruct((rows, width), bf16),
            jax.ShapeDtypeStruct((rows, width), bf16),
            jax.ShapeDtypeStruct((32, 128), f32),
        ],
        in_specs=[anywhere] * len(order) + [vmem] * 3,
        out_specs=[anywhere, anywhere, vmem],
        scratch_shapes=list(scratch.values()),
        compiler_params=pltpu.CompilerParams(**params),
    )(tokens, cotangent, *weights, adapter_a, adapter_b, scales, vecs, segments)


def per_device(
    mesh_shape,
    tokens,
    w_query,
    w_key,
    w_value,
    w_out,
    w_up,
    w_down,
    gain_one,
    shift_one,
    gain_two,
    shift_two,
    adapter_a,
    adapter_b,
    query_rank_scale,
    value_rank_scale,
    query_out_scale,
    value_out_scale,
    segments,
    cotangent,
):
    width = tokens.shape[1]
    rank_here = adapter_a.shape[1]
    ranks = rank_here * mesh_shape[1]
    out_scales = [query_out_scale.astype(f32), value_out_scale.astype(f32)]
    nothing = jnp.zeros((width,), f32)
    vecs = jnp.stack([gain_one, shift_one, gain_two, shift_two] + out_scales + [nothing, nothing])
    scales = jnp.stack([query_rank_scale, value_rank_scale])
    remote = mesh_shape == (8, 4)
    if not remote:
        adapter_a = lax.all_gather(adapter_a, "rank", axis=1, tiled=True)
        adapter_b = lax.all_gather(adapter_b, "rank", axis=0, tiled=True)
        scales = lax.all_gather(scales, "rank", axis=1, tiled=True)
        w_query, w_key, w_value, w_out, w_up, w_down = [
            lax.all_gather(w, "rows", axis=0, tiled=True)
            for w in (w_query, w_key, w_value, w_out, w_up, w_down)
        ]
        w_query = (w_query + dot(adapter_a * scales[0], adapter_b) * out_scales[0]).astype(bf16)
        w_value = (w_value + dot(adapter_a * scales[1], adapter_b) * out_scales[1]).astype(bf16)
    weights = [w_key, w_out, w_query, w_value, w_up, w_down]
    if not remote:
        weights = [w.reshape(4, 2, w.shape[0] // 8, w.shape[1]) for w in weights]
    scales = jnp.pad(scales, ((0, 14), (0, 0)))
    layer_out, input_grad, small = run_layer(
        remote, tokens, cotangent, weights, adapter_a, adapter_b, scales, vecs, segments
    )
    if not remote:
        small = lax.psum(small, ("rows", "rank"))
    small = small.reshape(-1)
    mine = lax.axis_index("rank") * rank_here
    return (
        layer_out,
        input_grad,
        lax.dynamic_slice(small, (mine,), (rank_here,)),
        lax.dynamic_slice(small, (ranks + mine,), (rank_here,)),
        small[2 * ranks : 2 * ranks + width],
        small[2 * ranks + width : 2 * ranks + 2 * width],
    )


def solution(mesh):
    return jax.shard_map(
        partial(per_device, (mesh.shape["rows"], mesh.shape["rank"])),
        mesh=mesh,
        in_specs=(
            P(("rows", "rank"), None),
            P("rows", None),
            P("rows", None),
            P("rows", None),
            P("rows", None),
            P("rows", None),
            P("rows", None),
            P(),
            P(),
            P(),
            P(),
            P(None, "rank"),
            P("rank", None),
            P("rank"),
            P("rank"),
            P(),
            P(),
            P(("rows", "rank"), None),
            P(("rows", "rank"), None),
        ),
        out_specs=(
            P(("rows", "rank"), None),
            P(("rows", "rank"), None),
            P("rank"),
            P("rank"),
            P(),
            P(),
        ),
        check_vma=False,
    )
```

```python
from functools import partial

import jax
import jax.numpy as jnp
from jax import lax
from jax.experimental import pallas as pl
from jax.experimental.pallas import tpu as pltpu
from jax.sharding import PartitionSpec as P

HEADS = 12
HEAD = 64
MESH = pl.DeviceIdType.MESH
epsilon = 1e-05
masked_score = -1e30
f32 = jnp.float32
bf16 = jnp.bfloat16
WINDOWS = ((0, 256), (0, 384), (128, 384), (256, 256))
AHEAD = 2
VMEM_LIMIT = 64 * 2**20


def dot(a, b):
    return jnp.dot(a, b, preferred_element_type=f32)


def dot_nt(a, b):
    return lax.dot_general(a, b, (((1,), (1,)), ((), ())), preferred_element_type=f32)


def dot_tn(a, b):
    return lax.dot_general(a, b, (((0,), (0,)), ((), ())), preferred_element_type=f32)


def flat(block):
    return block.reshape(block.shape[0] * block.shape[1] * block.shape[2], block.shape[3])


def mean(block):
    return jnp.mean(block, axis=1, keepdims=True)


def normalize(stream):
    centered = stream - mean(stream)
    inverse = lax.rsqrt(mean(centered * centered) + epsilon)
    return centered * inverse, inverse


def norm_backward(scaled, normed, inverse):
    return inverse * (scaled - mean(scaled) - normed * mean(scaled * normed))


def low_lanes():
    return lax.broadcasted_iota(jnp.int32, (128, 128), 1) < HEAD


def two_heads(block, low):
    zero = jnp.zeros_like(block)
    return jnp.concatenate([jnp.where(low, block, zero), jnp.where(low, zero, block)], axis=0)


class Links:
    def __init__(self, pieces, merged, ins, bufs, sems):
        self.pieces, self.merged, self.ins, self.bufs = pieces, merged, ins, bufs
        self.sems = sems
        self.row, self.rank = lax.axis_index("rows"), lax.axis_index("rank")
        self.z, self.x = self.row // 2, self.row % 2
        self.y, self.c = self.rank // 2, self.rank % 2
        z = self.z
        self.other = (z, z + 1 - 2 * (z % 2), (z + 2) % 4, 3 - z)
        self.middle = (z == 1) | (z == 2)
        self.to_z = [(self.other[d] * 2 + self.x, self.rank) for d in range(4)]
        self.to_x = (z * 2 + 1 - self.x, self.rank)
        self.to_y = (self.row, (1 - self.y) * 2 + self.c)
        self.to_core = (self.row, self.y * 2 + 1 - self.c)
        self.to_cross = (self.row, (1 - self.y) * 2 + 1 - self.c)
        self.rank_friends = [self.to_core, self.to_y, self.to_cross]
        self.row_friends = [
            (self.other[n // 2] * 2 + (self.x if n % 2 == 0 else 1 - self.x), self.rank)
            for n in range(1, 8)
        ]

    def greet(self):
        self.barrier = pltpu.get_barrier_semaphore()
        for friend in self.rank_friends + self.row_friends:
            pl.semaphore_signal(self.barrier, inc=1, device_id=friend, device_id_type=MESH)

    def meet(self):
        pl.semaphore_wait(self.barrier, len(self.rank_friends + self.row_friends))

    def wait_bytes(self, sem, rows, cols):
        ref = self.sems["ac"].at[pl.ds(0, rows), pl.ds(0, cols)]
        pltpu.make_async_copy(ref, ref, sem).wait()

    def copy(self, src, dst, send, recv, device):
        return pltpu.make_async_remote_copy(
            src_ref=src, dst_ref=dst, send_sem=send, recv_sem=recv,
            device_id=device, device_id_type=MESH,
        )

    def same(self, ref, send, recv, device):
        return self.copy(ref, ref, send, recv, device)

    def unit(self, p):
        return self.pieces[p][1] // 6

    def cols(self, p):
        return pl.ds(self.pieces[p][2], self.pieces[p][3])

    def plane_rows(self, p):
        u = self.unit(p)
        return pl.ds(pl.multiple_of(3 * u * self.c + u * self.y, 16), 2 * u)

    def side_rows(self, p, side):
        u = self.unit(p)
        return pl.ds(pl.multiple_of(3 * u * self.c + 2 * u * side, 16), u)

    def core_rows(self, p, core):
        u = self.unit(p)
        return pl.ds(pl.multiple_of(3 * u * core, 16), 3 * u)

    def buf(self, p):
        return self.bufs[self.pieces[p][0]]

    def is_merged(self, p):
        return self.pieces[p][0] in self.merged

    def at(self, p, z):
        return self.buf(p).at[z, self.x, self.plane_rows(p), self.cols(p)]

    def own(self, p):
        if self.is_merged(p):
            return self.at(p, self.z)
        return self.ins[self.pieces[p][0]].at[self.plane_rows(p), self.cols(p)]

    def local(self, p):
        return pltpu.make_async_copy(
            self.ins[self.pieces[p][0]].at[self.core_rows(p, self.c), self.cols(p)],
            self.buf(p).at[self.z, self.x, self.core_rows(p, self.c), self.cols(p)],
            self.sems["local"],
        )

    def z_send(self, p, d):
        return self.copy(
            self.own(p), self.at(p, self.z), self.sems["sz"].at[d // 3], self.sems["rz"].at[p, d - 1],
            self.to_z[d],
        )

    def z_pass(self, p):
        return self.same(
            self.at(p, self.other[2]), self.sems["sz"].at[1], self.sems["rz"].at[p, 2], self.to_z[1]
        )

    def z_recv(self, p, d):
        return self.same(
            self.at(p, self.other[d]), self.sems["sz"].at[0], self.sems["rz"].at[p, d - 1], self.to_z[d]
        )

    def x_send(self, p, d):
        src = self.own(p) if d == 0 else self.at(p, self.other[d])
        return self.copy(
            src, self.at(p, self.other[d]), self.sems["sx"], self.sems["rx"].at[p], self.to_x
        )

    def x_recv(self, p):
        ref = self.buf(p).at[:, 1 - self.x, self.plane_rows(p), self.cols(p)]
        return self.same(ref, self.sems["sx"], self.sems["rx"].at[p], self.to_x)

    def y_one(self, p, d):
        ref = self.buf(p).at[self.other[d], self.x, self.side_rows(p, self.y), self.cols(p)]
        send = self.sems["sy"].at[0] if d > 0 else self.sems["sq"].at[self.pieces[p][0] - 2]
        return self.same(ref, send, self.sems["ry"].at[p], self.to_y)

    def y_many(self, p):
        ref = self.buf(p).at[:, 1 - self.x, self.side_rows(p, self.y), self.cols(p)]
        return self.same(ref, self.sems["sy"].at[0], self.sems["ry"].at[p], self.to_y)

    def core_copy(self, p, core):
        ref = self.buf(p).at[:, :, self.core_rows(p, core), self.cols(p)]
        first = 0 if self.pieces[p][0] < 5 else 1
        return self.same(ref, self.sems["sk"].at[first], self.sems["rk"].at[p], self.to_core)

    def launch(self, p):
        self.z_send(p, 2).start()
        self.z_send(p, 1).start()
        pl.when(self.middle)(lambda: self.z_send(p, 3).start())
        self.x_send(p, 0).start()

    def stage_z(self, p):
        if self.is_merged(p):
            self.y_one(p, 0).start()
        for d in (2, 1, 3):
            self.z_recv(p, d).wait_recv()
            if d == 2:
                pl.when(self.middle)(lambda: self.z_pass(p).start())
            self.x_send(p, d).start()
            self.y_one(p, d).start()

    def stage_x(self, p):
        self.x_recv(p).wait_recv()
        self.y_many(p).start()

    def stage_y(self, p):
        units = 8 if self.is_merged(p) else 7
        self.wait_bytes(self.sems["ry"].at[p], units * self.unit(p), self.pieces[p][3])
        self.core_copy(p, self.c).start()

    def tick(self, t, between):
        total = len(self.pieces)
        if t < total:
            self.stage_z(t)
        if t + AHEAD < total:
            self.launch(t + AHEAD)
        between(t, 0)
        if 0 <= t - 1 < total:
            self.stage_x(t - 1)
        between(t, 1)
        if 0 <= t - 2 < total:
            self.stage_y(t - 2)
        if 0 <= t - 3 < total:
            self.core_copy(t - 3, 1 - self.c).wait_recv()
        between(t, 2)

    def drain(self):
        units = sum(self.unit(p) * self.pieces[p][3] for p in range(len(self.pieces)))
        hidden = self.sems["ac"].shape[1]
        self.wait_bytes(self.sems["sz"].at[0], 4 * units // hidden, hidden)
        pl.when(self.middle)(lambda: self.wait_bytes(self.sems["sz"].at[1], 4 * units // hidden, hidden))
        self.wait_bytes(self.sems["sx"], 8 * units // hidden, hidden)
        self.wait_bytes(self.sems["sy"].at[0], 7 * units // hidden, hidden)
        for p in range(len(self.pieces)):
            if self.is_merged(p):
                self.y_one(p, 0).wait_send()
        for n in range(2):
            own = [p for p in range(len(self.pieces)) if (self.pieces[p][0] == 5) == (n == 1)]
            size = sum(self.unit(p) * self.pieces[p][3] for p in own)
            self.wait_bytes(self.sems["sk"].at[n], 24 * size // hidden, hidden)


def layer_kernel(remote, pieces, names, *refs):
    r = dict(zip(names, refs))
    tok, cot, mix, hb, acc = r["tok"], r["cot"], r["mix"], r["hb"], r["acc"]
    q, k, v, ac = r["q"], r["k"], r["v"], r["ac"]
    slopes = [r["slope%d" % n] for n in range(4)]
    fa, fb, fs = r["fa"], r["fb"], r["fs"]
    weights = [r[name] for name in ("wk", "wo", "wq", "wv", "wu", "wd")]
    wk, wo, wq, wv, wu, wd = weights
    ins = [r[name + "_in"] for name in ("wk", "wo", "wq", "wv", "wu", "wd")]
    width = tok.shape[1]
    rows = tok.shape[0]
    hidden = ac.shape[1]
    halves = [pl.ds(n * (rows // 2), rows // 2) for n in range(2)]
    chunks = [pl.ds(n * width, width) for n in range(hidden // width)]
    gain_one, shift_one, gain_two, shift_two = [
        r[name][...].reshape(1, width) for name in ("gain_one", "shift_one", "gain_two", "shift_two")
    ]
    scale_outs = [r[name][...].astype(f32).reshape(1, width) for name in ("scale_q", "scale_v")]

    def load(src, dst, n):
        return pltpu.make_async_copy(src, dst, r["load"].at[n])

    load_tok, load_cot = load(r["tok_in"], tok, 0), load(r["cot_in"], cot, 1)
    load_tok.start()
    load_cot.start()
    if remote:
        links = Links(pieces, (2, 3), ins, weights, r)
        row, rank = links.row, links.rank
        mine = pl.ds(pl.multiple_of(rank * 256, 256), 256)
        a_rows = load(r["fa_in"].at[pl.ds(pl.multiple_of(row * 96, 96), 96), :], r["a_rows"], 4)
        adapter = [
            load(r["fb_in"], fb.at[mine, :], 3),
            load(r["fa_in"], fa.at[:, mine], 2),
            load(ins[2].at[links.plane_rows(2), :], r["own_qv"].at[0], 5),
            load(ins[3].at[links.plane_rows(3), :], r["own_qv"].at[1], 6),
        ]
        a_rows.start()
        for copy in adapter:
            copy.start()
        links.greet()
        for p in range(len(pieces)):
            if not links.is_merged(p):
                links.local(p).start()
        rank_scales = [r[name][...].astype(f32).reshape(1, 256) for name in ("rank_q", "rank_v")]
        fs[:, mine] = jnp.concatenate(rank_scales + [jnp.zeros((14, 256), f32)], axis=0).astype(bf16)
        part, met = r["part"], r["met"]
        a_rows.wait()
        adapter[0].wait()
        b_rows = fb[mine, :]
        for n in range(2):
            scaled = r["a_rows"][...].astype(f32) * rank_scales[n]
            part[n] = dot(scaled.astype(bf16), b_rows).astype(bf16)
    else:
        adapter = [load(r[n + "_in"], r[n], 2 + i) for i, n in enumerate(("fa", "fb", "fs"))]
        adapter += [load(src, dst, 5 + i) for i, (src, dst) in enumerate(zip(ins, weights))]
        for copy in adapter:
            copy.start()
        for copy in adapter:
            copy.wait()

    bias, probs = [r["bias%d" % t] for t in range(4)], [r["probs%d" % t] for t in range(4)]
    segs = r["segs"][...].astype(f32)
    padded = jnp.concatenate([segs, jnp.zeros((14, segs.shape[1]), f32)], axis=0).astype(bf16)
    for b in range(2):
        pick = (lax.broadcasted_iota(jnp.int32, (16, 128), 0) == b).astype(f32).astype(bf16)
        column = dot_tn(padded, pick)
        for t, (start, size) in enumerate(WINDOWS):
            same = column[start : start + size, :] == segs[b : b + 1, 128 * t : 128 * t + 128]
            bias[t][b] = jnp.where(same, 0.0, masked_score)
    low = low_lanes()

    if remote:

        def part_rows(y, c):
            return pl.ds(pl.multiple_of(48 * c + 16 * y, 16), 32)

        places = (
            (links.y, 1 - links.c), (1 - links.y, links.c), (1 - links.y, 1 - links.c)
        )
        parts = [
            links.copy(
                part.at[:, part_rows(*place), :], met.at[n], r["sm"].at[n], r["rm"].at[n],
                links.rank_friends[n],
            )
            for n, place in enumerate(places)
        ]
        links.meet()
        for copy in parts:
            copy.start()
        for p in range(AHEAD):
            links.launch(p)
        load_tok.wait()
        for copy in adapter[1:]:
            copy.wait()
        local_units = sum(
            3 * links.unit(p) * pieces[p][3] for p in range(len(pieces)) if not links.is_merged(p)
        )
        links.wait_bytes(r["local"], local_units // width, width)
        for copy in parts:
            copy.wait_recv()
        for n, buf in enumerate((wq, wv)):
            total = part[n, part_rows(links.y, links.c), :].astype(f32)
            for slot in range(3):
                total = total + met[slot, n].astype(f32)
            joined = r["own_qv"][n].astype(f32) + total * scale_outs[n]
            buf[links.z, links.x, links.plane_rows(2 + n), :] = joined.astype(bf16)
    else:
        load_tok.wait()

    def project(weight, out, scale):
        out[...] = (dot(tok[...], flat(weight[...])) * scale).astype(bf16)

    def attend(b, first):
        for p in range(first, first + 3):
            lanes = pl.ds(128 * p, 128)
            for t, (start, size) in enumerate(WINDOWS):
                here = pl.ds(pl.multiple_of(b * 512 + 128 * t, 128), 128)
                window = pl.ds(pl.multiple_of(b * 512 + start, 128), size)
                scores = dot_nt(k[window, lanes], two_heads(q[here, lanes], low))
                mask = bias[t][b]
                scores = jnp.where(jnp.concatenate([mask, mask], axis=1) < 0.0, masked_score, scores)
                weight = jnp.exp(scores - jnp.max(scores, axis=0, keepdims=True))
                weight = weight * (1.0 / jnp.sum(weight, axis=0, keepdims=True))
                attention = weight.astype(bf16)
                probs[t][b * (HEADS // 2) + p] = attention
                both = dot_tn(attention, v[window, lanes])
                mix[here, lanes] = jnp.where(low, both[:128], both[128:]).astype(bf16)

    def first_norm(n):
        for half in halves[n : n + 1]:
            stream = tok[half, :].astype(f32) + dot(mix[half, :], flat(wo[...]))
            normed, inverse = normalize(stream)
            r["n1"][half, :] = normed.astype(bf16)
            r["i1"][half, :] = inverse
            out = normed * gain_one + shift_one
            acc[half, :] = out
            hb[half, :] = out.astype(bf16)

    def up(n):
        proj = dot(hb[...], flat(wu[:, :, :, chunks[n]]))
        bell = jnp.exp(proj * proj * -0.5)
        area = 0.5 + 0.5 * lax.erf(proj * 0.7071067811865476)
        ac[:, chunks[n]] = (proj * area).astype(bf16)
        slopes[n][...] = (area + proj * bell * 0.3989422804014327).astype(bf16)

    third = pl.ds(0, width // 3), pl.ds(width // 3, width // 3), pl.ds(2 * (width // 3), width // 3)

    def down(n):
        acc[:, third[n]] = acc[:, third[n]] + dot(ac[...], flat(wd[:, :, :, third[n]]))

    send_out = [
        pltpu.make_async_copy(r["lo"].at[half, :], r["out"].at[half, :], r["store"].at[n])
        for n, half in enumerate(halves)
    ]

    def second_norm():
        for n, half in enumerate(halves):
            normed, inverse = normalize(acc[half, :])
            r["lo"][half, :] = (normed * gain_two + shift_two).astype(bf16)
            send_out[n].start()
            grad = norm_backward(cot[half, :].astype(f32) * gain_two, normed, inverse)
            acc[half, :] = grad
            hb[half, :] = grad.astype(bf16)

    steps = {
        (3, 2): [lambda: project(wk, k, 1.0)],
        (5, 2): [lambda: project(wq, q, 0.125)],
        (6, 2): [lambda: project(wv, v, 1.0)],
        (7, 0): [lambda: attend(0, 0)],
        (7, 2): [lambda: attend(0, 3)],
        (8, 0): [lambda: attend(1, 0)],
        (8, 2): [lambda: attend(1, 3)],
        (9, 0): [lambda: first_norm(0)],
        (9, 1): [lambda: first_norm(1)],
        (9, 2): [lambda: up(0)],
        (10, 0): [lambda: up(1)],
        (10, 2): [lambda: up(2)],
        (11, 0): [lambda: up(3)],
        (11, 2): [lambda: down(0)],
        (12, 2): [lambda: down(1)],
        (13, 2): [lambda: down(2)],
    }

    def between(t, phase):
        for step in steps.get((t, phase), ()):
            step()

    if remote:
        own_adapter = (fa.at[:, mine], fb.at[mine, :], fs.at[:, mine])
        theirs = pl.ds(pl.multiple_of(((1 - links.y) * 2 + links.c) * 256, 256), 256)
        got_adapter = (fa.at[:, theirs], fb.at[theirs, :], fs.at[:, theirs])
        core = pl.ds(pl.multiple_of((links.y * 2 + 1 - links.c) * 256, 256), 256)
        core_adapter = (fa.at[:, core], fb.at[core, :], fs.at[:, core])
        cross = pl.ds(pl.multiple_of(((1 - links.y) * 2 + 1 - links.c) * 256, 256), 256)
        cross_adapter = (fa.at[:, cross], fb.at[cross, :], fs.at[:, cross])

        def adapters(refs_, n, device):
            return [links.same(ref, r["sa"].at[n, i], r["ra"].at[n, i], device) for i, ref in enumerate(refs_)]

        for t in range(len(pieces) + 3):
            links.tick(t, between)
            if t == len(pieces):
                for copy in adapters(own_adapter, 0, links.to_y) + adapters(own_adapter, 1, links.to_core):
                    copy.start()
    else:
        for t in range(len(pieces) + 3):
            for phase in range(3):
                between(t, phase)
    load_cot.wait()
    second_norm()
    if remote:
        links.drain()
        for copy in parts:
            copy.wait_send()

    for n in range(hidden // width):
        grad = dot_nt(hb[...], wd[n].reshape(width, width))
        ac[:, chunks[n]] = (grad * slopes[n][...].astype(f32)).astype(bf16)
    if remote:
        for copy in adapters(got_adapter, 0, links.to_y):
            copy.wait_recv()
        passing = adapters(got_adapter, 2, links.to_core)
        for copy in passing:
            copy.start()
    for half in halves:
        grad = acc[half, :] + dot_nt(ac[half, :], flat(wu[...]))
        grad = norm_backward(grad * gain_one, r["n1"][half, :].astype(f32), r["i1"][half, :])
        acc[half, :] = grad
        hb[half, :] = grad.astype(bf16)
    grad_mix, grad_q, grad_k, grad_v = slopes
    heads = lax.broadcasted_iota(jnp.int32, (16, width), 1) // HEAD
    pick = (heads == lax.broadcasted_iota(jnp.int32, (16, width), 0)).astype(f32).astype(bf16)
    grad = dot_nt(hb[...], flat(wo[...]))
    grad_mix[...] = grad.astype(bf16)
    r["delta"][...] = dot_nt(pick, (grad * mix[...].astype(f32)).astype(bf16))
    delta = r["delta"]

    def attend_back(b, _):
        for p in range(HEADS // 2):
            lanes = pl.ds(128 * p, 128)
            keys, vals = [None] * 4, [None] * 4
            for t, (start, size) in enumerate(WINDOWS):
                here = pl.ds(pl.multiple_of(b * 512 + 128 * t, 128), 128)
                window = pl.ds(pl.multiple_of(b * 512 + start, 128), size)
                grad_pair = two_heads(grad_mix[here, lanes], low)
                grad_attn = dot_nt(v[window, lanes], grad_pair)
                attention = probs[t][b * (HEADS // 2) + p]
                centre = jnp.concatenate(
                    [delta[2 * p : 2 * p + 1, here], delta[2 * p + 1 : 2 * p + 2, here]], axis=1
                )
                grad_scores = (attention.astype(f32) * (grad_attn - centre)).astype(bf16)
                both = dot_tn(grad_scores, k[window, lanes])
                both = jnp.where(low, both[:128], both[128:]) * 0.125
                grad_q[here, lanes] = both.astype(bf16)
                key_part = dot(grad_scores, two_heads(q[here, lanes], low))
                val_part = dot(attention, grad_pair)
                for total, piece in ((keys, key_part), (vals, val_part)):
                    for n in range(size // 128):
                        at = start // 128 + n
                        add = piece[128 * n : 128 * n + 128]
                        total[at] = add if total[at] is None else total[at] + add
            for t in range(4):
                here = pl.ds(pl.multiple_of(b * 512 + 128 * t, 128), 128)
                grad_k[here, lanes] = keys[t].astype(bf16)
                grad_v[here, lanes] = vals[t].astype(bf16)
        return 0

    lax.fori_loop(0, 2, attend_back, 0)

    square = pl.ds(0, width)
    grads = jnp.concatenate([grad_q[...], grad_v[...]], axis=1)
    ac[square, pl.ds(0, 2 * width)] = dot_tn(tok[...], grads).astype(bf16)
    if remote:
        for refs_, n in ((core_adapter, 1), (cross_adapter, 2)):
            for copy in adapters(refs_, n, links.to_core):
                copy.wait_recv()
    for n in range(2):
        ac[:, chunks[2 + n]] = (dot_tn(fa[...], ac[square, chunks[n]]) * fb[...].astype(f32)).astype(bf16)
    out_scales = jnp.concatenate(scale_outs + [jnp.zeros((14, width), f32)], axis=0).astype(bf16)
    red = r["red"]
    red[28:32, :] = jnp.zeros((4, 128), f32)
    for n in range(2):
        along_rank = dot_nt(out_scales, ac[:, chunks[2 + n]])
        along_width = dot(fs[...], ac[:, chunks[2 + n]])
        for i in range(8):
            red[8 * n + i : 8 * n + i + 1, :] = along_rank[n : n + 1, 128 * i : 128 * i + 128]
        for i in range(6):
            at = 16 + 6 * n + i
            red[at : at + 1, :] = along_width[n : n + 1, 128 * i : 128 * i + 128]
    if remote:
        one, two = r["one"], r["two"]
        one[rank] = red[...]
        first = [
            links.copy(red, one.at[rank], r["s1"].at[n], r["r1"].at[n], friend)
            for n, friend in enumerate(links.rank_friends)
        ]
        for copy in first:
            copy.start()
    acc[...] = acc[...] + dot_nt(grad_k[...], flat(wk[...]))
    if remote:
        for copy in first:
            copy.wait_recv()
        r["sum"][...] = (one[0] + one[1]) + (one[2] + one[3])
        two[row] = r["sum"][...]
        second = [
            links.copy(r["sum"], two.at[row], r["s2"].at[n], r["r2"].at[n], friend)
            for n, friend in enumerate(links.row_friends)
        ]
        for copy in second:
            copy.start()
    send_grad = [
        pltpu.make_async_copy(cot.at[half, :], r["grad"].at[half, :], r["store"].at[2 + n])
        for n, half in enumerate(halves)
    ]
    for n, half in enumerate(halves):
        grad = acc[half, :] + dot_nt(grad_q[half, :], flat(wq[...]))
        grad = grad + dot_nt(grad_v[half, :], flat(wv[...]))
        cot[half, :] = grad.astype(bf16)
        send_grad[n].start()
    if remote:
        for copy in second:
            copy.wait_recv()
        total = two[0]
        for n in range(1, 8):
            total = total + two[n]
        for n, name in enumerate(("rank_grad_q", "rank_grad_v")):
            for i in range(2):
                line = jnp.zeros((1, 128), f32)
                for place in range(4):
                    at = 8 * n + 2 * place + i
                    line = jnp.where(rank == place, total[at : at + 1, :], line)
                r[name][pl.ds(128 * i, 128)] = line.reshape(128)
        for n, name in enumerate(("out_grad_q", "out_grad_v")):
            for i in range(6):
                at = 16 + 6 * n + i
                r[name][pl.ds(128 * i, 128)] = total[at : at + 1, :].reshape(128)
        for copy in first + second + passing:
            copy.wait_send()
        for copy in adapters(own_adapter, 0, links.to_y) + adapters(own_adapter, 1, links.to_core):
            copy.wait_send()
    else:
        r["small"][...] = red[...]
    for copy in send_out + send_grad:
        copy.wait()


def run_layer(remote, tokens, cotangent, weights, adapter_a, adapter_b, scales, vectors, segments):
    rows, width = tokens.shape
    hidden = weights[4].shape[-1]
    ranks = 1024
    sem = pltpu.SemaphoreType.DMA
    pieces = [(m, 96, 0, width) for m in range(4)]
    pieces += [(4, 96, n * width, width) for n in range(hidden // width)]
    pieces += [(5, 384, n * (width // 3), width // 3) for n in range(3)]
    total = len(pieces)
    block = (4, 2, width // 8, width)
    scratch = {
        "tok": pltpu.VMEM((rows, width), bf16),
        "cot": pltpu.VMEM((rows, width), bf16),
        "wk": pltpu.VMEM(block, bf16),
        "wo": pltpu.VMEM(block, bf16),
        "wq": pltpu.VMEM(block, bf16),
        "wv": pltpu.VMEM(block, bf16),
        "wu": pltpu.VMEM((4, 2, width // 8, hidden), bf16),
        "wd": pltpu.VMEM((4, 2, hidden // 8, width), bf16),
        "fa": pltpu.VMEM((width, ranks), bf16),
        "fb": pltpu.VMEM((ranks, width), bf16),
        "fs": pltpu.VMEM((16, ranks), bf16),
        "q": pltpu.VMEM((rows, width), bf16),
        "k": pltpu.VMEM((rows, width), bf16),
        "v": pltpu.VMEM((rows, width), bf16),
        "mix": pltpu.VMEM((rows, width), bf16),
        "n1": pltpu.VMEM((rows, width), bf16),
        "i1": pltpu.VMEM((rows, 1), f32),
        "hb": pltpu.VMEM((rows, width), bf16),
        "lo": pltpu.VMEM((rows, width), bf16),
        "ac": pltpu.VMEM((rows, hidden), bf16),
        "acc": pltpu.VMEM((rows, width), f32),
        "delta": pltpu.VMEM((16, rows), f32),
        "red": pltpu.VMEM((32, 128), f32),
        "load": sem((11,)),
        "store": sem((4,)),
    }
    for n in range(hidden // width):
        scratch["slope%d" % n] = pltpu.VMEM((rows, width), bf16)
    for t, (_, size) in enumerate(WINDOWS):
        scratch["bias%d" % t] = pltpu.VMEM((2, size, 128), f32)
        scratch["probs%d" % t] = pltpu.VMEM((HEADS, size, 256), bf16)
    if remote:
        scratch.update({
            "a_rows": pltpu.VMEM((96, 256), bf16),
            "own_qv": pltpu.VMEM((2, 32, width), bf16),
            "part": pltpu.VMEM((2, 96, width), bf16),
            "met": pltpu.VMEM((3, 2, 32, width), bf16),
            "one": pltpu.VMEM((4, 32, 128), f32),
            "two": pltpu.VMEM((8, 32, 128), f32),
            "sum": pltpu.VMEM((32, 128), f32),
            "local": sem(()),
            "sz": sem((2,)),
            "rz": sem((total, 3)),
            "sx": sem(()),
            "rx": sem((total,)),
            "sy": sem((1,)),
            "ry": sem((total,)),
            "sq": sem((2,)),
            "sk": sem((2,)),
            "rk": sem((total,)),
            "sm": sem((3,)),
            "rm": sem((3,)),
            "sa": sem((3, 3)),
            "ra": sem((3, 3)),
            "s1": sem((3,)),
            "r1": sem((3,)),
            "s2": sem((7,)),
            "r2": sem((7,)),
        })
    order = ["tok_in", "cot_in", "wk_in", "wo_in", "wq_in", "wv_in", "wu_in", "wd_in", "fa_in", "fb_in"]
    given = ["gain_one", "shift_one", "gain_two", "shift_two", "scale_q", "scale_v", "segs"]
    outs = {"out": ((rows, width), bf16), "grad": ((rows, width), bf16)}
    if remote:
        given += ["rank_q", "rank_v"]
        here = ranks // 4
        outs.update({"rank_grad_q": ((here,), f32), "rank_grad_v": ((here,), f32)})
        outs.update({"out_grad_q": ((width,), f32), "out_grad_v": ((width,), f32)})
        operands = vectors + [segments] + scales
    else:
        order += ["fs_in"]
        outs["small"] = ((32, 128), f32)
        operands = scales + vectors + [segments]
    names = order + given + list(outs) + list(scratch)
    anywhere, vmem = pl.BlockSpec(memory_space=pl.ANY), pl.BlockSpec(memory_space=pltpu.VMEM)
    params = dict(vmem_limit_bytes=VMEM_LIMIT, has_side_effects=True)
    if remote:
        params["collective_id"] = 0
    return pl.pallas_call(
        partial(layer_kernel, remote, pieces, names),
        out_shape=[jax.ShapeDtypeStruct(*out) for out in outs.values()],
        in_specs=[anywhere] * len(order) + [vmem] * len(given),
        out_specs=[anywhere, anywhere] + [vmem] * (len(outs) - 2),
        scratch_shapes=list(scratch.values()),
        compiler_params=pltpu.CompilerParams(**params),
    )(tokens, cotangent, *weights, adapter_a, adapter_b, *operands)


def per_device(
    mesh_shape,
    tokens,
    w_query,
    w_key,
    w_value,
    w_out,
    w_up,
    w_down,
    gain_one,
    shift_one,
    gain_two,
    shift_two,
    adapter_a,
    adapter_b,
    query_rank_scale,
    value_rank_scale,
    query_out_scale,
    value_out_scale,
    segments,
    cotangent,
):
    vectors = [gain_one, shift_one, gain_two, shift_two, query_out_scale, value_out_scale]
    weights = [w_key, w_out, w_query, w_value, w_up, w_down]
    scales = [query_rank_scale, value_rank_scale]
    if mesh_shape == (8, 4):
        return tuple(
            run_layer(True, tokens, cotangent, weights, adapter_a, adapter_b, scales, vectors, segments)
        )
    width = tokens.shape[1]
    rank_here = adapter_a.shape[1]
    ranks = rank_here * mesh_shape[1]
    adapter_a = lax.all_gather(adapter_a, "rank", axis=1, tiled=True)
    adapter_b = lax.all_gather(adapter_b, "rank", axis=0, tiled=True)
    scales = lax.all_gather(jnp.stack(scales), "rank", axis=1, tiled=True)
    weights = [lax.all_gather(w, "rows", axis=0, tiled=True) for w in weights]
    for n in range(2):
        added = dot(adapter_a * scales[n], adapter_b) * vectors[4 + n].astype(f32)
        weights[2 + n] = (weights[2 + n] + added).astype(bf16)
    weights = [w.reshape(4, 2, w.shape[0] // 8, w.shape[1]) for w in weights]
    scales = [jnp.pad(scales, ((0, 14), (0, 0)))]
    layer_out, input_grad, small = run_layer(
        False, tokens, cotangent, weights, adapter_a, adapter_b, scales, vectors, segments
    )
    small = lax.psum(small, ("rows", "rank")).reshape(-1)
    mine = lax.axis_index("rank") * rank_here
    return (
        layer_out,
        input_grad,
        lax.dynamic_slice(small, (mine,), (rank_here,)),
        lax.dynamic_slice(small, (ranks + mine,), (rank_here,)),
        small[2 * ranks : 2 * ranks + width],
        small[2 * ranks + width : 2 * ranks + 2 * width],
    )


def solution(mesh):
    return jax.shard_map(
        partial(per_device, (mesh.shape["rows"], mesh.shape["rank"])),
        mesh=mesh,
        in_specs=(
            P(("rows", "rank"), None),
            P("rows", None),
            P("rows", None),
            P("rows", None),
            P("rows", None),
            P("rows", None),
            P("rows", None),
            P(),
            P(),
            P(),
            P(),
            P(None, "rank"),
            P("rank", None),
            P("rank"),
            P("rank"),
            P(),
            P(),
            P(("rows", "rank"), None),
            P(("rows", "rank"), None),
        ),
        out_specs=(
            P(("rows", "rank"), None),
            P(("rows", "rank"), None),
            P("rank"),
            P("rank"),
            P(),
            P(),
        ),
        check_vma=False,
    )
```

```python
from functools import partial

import jax
import jax.numpy as jnp
from jax import lax
from jax.experimental import pallas as pl
from jax.experimental.pallas import tpu as pltpu
from jax.sharding import PartitionSpec as P

HEADS = 12
HEAD = 64
MESH = pl.DeviceIdType.MESH
epsilon = 1e-05
masked_score = -1e30
f32 = jnp.float32
bf16 = jnp.bfloat16
WINDOWS = ((0, 256), (0, 384), (128, 384), (256, 256))
AHEAD = 2
VMEM_LIMIT = 64 * 2**20


def dot(a, b):
    return jnp.dot(a, b, preferred_element_type=f32)


def dot_nt(a, b):
    return lax.dot_general(a, b, (((1,), (1,)), ((), ())), preferred_element_type=f32)


def dot_tn(a, b):
    return lax.dot_general(a, b, (((0,), (0,)), ((), ())), preferred_element_type=f32)


def flat(block):
    return block.reshape(block.shape[0] * block.shape[1] * block.shape[2], block.shape[3])


def mean(block):
    return jnp.mean(block, axis=1, keepdims=True)


def normalize(stream):
    centered = stream - mean(stream)
    inverse = lax.rsqrt(mean(centered * centered) + epsilon)
    return centered * inverse, inverse


def norm_backward(scaled, normed, inverse):
    return inverse * (scaled - mean(scaled) - normed * mean(scaled * normed))


def low_lanes():
    return lax.broadcasted_iota(jnp.int32, (128, 128), 1) < HEAD


def two_heads(block, low):
    zero = jnp.zeros_like(block)
    return jnp.concatenate([jnp.where(low, block, zero), jnp.where(low, zero, block)], axis=0)


class Links:
    def __init__(self, pieces, merged, ins, bufs, sems):
        self.pieces, self.merged, self.ins, self.bufs = pieces, merged, ins, bufs
        self.sems = sems
        self.row, self.rank = lax.axis_index("rows"), lax.axis_index("rank")
        self.z, self.x = self.row // 2, self.row % 2
        self.y, self.c = self.rank // 2, self.rank % 2
        z = self.z
        self.other = (z, z + 1 - 2 * (z % 2), (z + 2) % 4, 3 - z)
        self.middle = (z == 1) | (z == 2)
        self.to_z = [(self.other[d] * 2 + self.x, self.rank) for d in range(4)]
        self.to_x = (z * 2 + 1 - self.x, self.rank)
        self.to_y = (self.row, (1 - self.y) * 2 + self.c)
        self.to_core = (self.row, self.y * 2 + 1 - self.c)
        self.to_cross = (self.row, (1 - self.y) * 2 + 1 - self.c)
        self.rank_friends = [self.to_core, self.to_y, self.to_cross]
        self.row_friends = [
            (self.other[n // 2] * 2 + (self.x if n % 2 == 0 else 1 - self.x), self.rank)
            for n in range(1, 8)
        ]

    def greet(self):
        self.barrier = pltpu.get_barrier_semaphore()
        for friend in self.rank_friends + self.row_friends:
            pl.semaphore_signal(self.barrier, inc=1, device_id=friend, device_id_type=MESH)

    def meet(self):
        pl.semaphore_wait(self.barrier, len(self.rank_friends + self.row_friends))

    def wait_bytes(self, sem, rows, cols):
        ref = self.sems["ac"].at[pl.ds(0, rows), pl.ds(0, cols)]
        pltpu.make_async_copy(ref, ref, sem).wait()

    def copy(self, src, dst, send, recv, device):
        return pltpu.make_async_remote_copy(
            src_ref=src, dst_ref=dst, send_sem=send, recv_sem=recv,
            device_id=device, device_id_type=MESH,
        )

    def same(self, ref, send, recv, device):
        return self.copy(ref, ref, send, recv, device)

    def unit(self, p):
        return self.pieces[p][1] // 6

    def cols(self, p):
        return pl.ds(self.pieces[p][2], self.pieces[p][3])

    def plane_rows(self, p):
        u = self.unit(p)
        return pl.ds(pl.multiple_of(3 * u * self.c + u * self.y, 16), 2 * u)

    def side_rows(self, p, side):
        u = self.unit(p)
        return pl.ds(pl.multiple_of(3 * u * self.c + 2 * u * side, 16), u)

    def core_rows(self, p, core):
        u = self.unit(p)
        return pl.ds(pl.multiple_of(3 * u * core, 16), 3 * u)

    def buf(self, p):
        return self.bufs[self.pieces[p][0]]

    def is_merged(self, p):
        return self.pieces[p][0] in self.merged

    def at(self, p, z):
        return self.buf(p).at[z, self.x, self.plane_rows(p), self.cols(p)]

    def own(self, p):
        if self.is_merged(p):
            return self.at(p, self.z)
        return self.ins[self.pieces[p][0]].at[self.plane_rows(p), self.cols(p)]

    def local(self, p):
        return pltpu.make_async_copy(
            self.ins[self.pieces[p][0]].at[self.core_rows(p, self.c), self.cols(p)],
            self.buf(p).at[self.z, self.x, self.core_rows(p, self.c), self.cols(p)],
            self.sems["local"],
        )

    def z_send(self, p, d):
        return self.copy(
            self.own(p), self.at(p, self.z), self.sems["sz"].at[d // 3], self.sems["rz"].at[p, d - 1],
            self.to_z[d],
        )

    def z_pass(self, p):
        return self.same(
            self.at(p, self.other[2]), self.sems["sz"].at[1], self.sems["rz"].at[p, 2], self.to_z[1]
        )

    def z_recv(self, p, d):
        return self.same(
            self.at(p, self.other[d]), self.sems["sz"].at[0], self.sems["rz"].at[p, d - 1], self.to_z[d]
        )

    def common_rows(self, p):
        u = self.unit(p)
        return pl.ds(pl.multiple_of(3 * u * self.c + u, 16), u)

    def x_send(self, p, d):
        if d == 1:
            ref = self.buf(p).at[self.other[1], self.x, self.side_rows(p, self.y), self.cols(p)]
            return self.same(ref, self.sems["sx"].at[0], self.sems["rx"].at[p], self.to_x)
        src = self.own(p) if d == 0 else self.at(p, self.other[d])
        recv = self.sems["rw"].at[p, 0] if d == 0 else self.sems["rx"].at[p]
        return self.copy(src, self.at(p, self.other[d]), self.sems["sx"].at[0], recv, self.to_x)

    def x_own_recv(self, p):
        ref = self.buf(p).at[self.z, 1 - self.x, self.plane_rows(p), self.cols(p)]
        return self.same(ref, self.sems["sx"].at[0], self.sems["rw"].at[p, 0], self.to_x)

    def z_extra(self, p, d):
        ref = self.buf(p).at[self.other[d], 1 - self.x, self.common_rows(p), self.cols(p)]
        return self.same(ref, self.sems["sx"].at[1], self.sems["rw"].at[p, 1], self.to_z[1])

    def y_one(self, p, d):
        ref = self.buf(p).at[self.other[d], self.x, self.side_rows(p, self.y), self.cols(p)]
        send = self.sems["sy"].at[0] if d > 0 else self.sems["sq"].at[self.pieces[p][0] - 2]
        return self.same(ref, send, self.sems["ry"].at[p], self.to_y)

    def y_many(self, p):
        ref = self.buf(p).at[:, 1 - self.x, self.side_rows(p, self.y), self.cols(p)]
        return self.same(ref, self.sems["sy"].at[0], self.sems["ry"].at[p], self.to_y)

    def core_copy(self, p, core):
        ref = self.buf(p).at[:, :, self.core_rows(p, core), self.cols(p)]
        first = 0 if self.pieces[p][0] < 5 else 1
        return self.same(ref, self.sems["sk"].at[first], self.sems["rk"].at[p], self.to_core)

    def launch(self, p):
        self.z_send(p, 2).start()
        self.z_send(p, 1).start()
        pl.when(self.middle)(lambda: self.z_send(p, 3).start())
        self.x_send(p, 0).start()

    def stage_z(self, p):
        if self.is_merged(p):
            self.y_one(p, 0).start()
        for d in (2, 1, 3):
            self.z_recv(p, d).wait_recv()
            if d == 2:
                pl.when(self.middle)(lambda: self.z_pass(p).start())
            self.x_send(p, d).start()
            self.y_one(p, d).start()
        self.x_own_recv(p).wait_recv()
        self.z_extra(p, 0).start()

    def stage_x(self, p):
        self.wait_bytes(self.sems["rx"].at[p], 5 * self.unit(p), self.pieces[p][3])
        self.y_many(p).start()

    def stage_y(self, p):
        units = 8 if self.is_merged(p) else 7
        self.wait_bytes(self.sems["ry"].at[p], units * self.unit(p), self.pieces[p][3])
        self.z_extra(p, 1).wait_recv()
        self.core_copy(p, self.c).start()

    def tick(self, t, between):
        total = len(self.pieces)
        if t < total:
            self.stage_z(t)
        between(t, 0)
        if t + AHEAD < total:
            self.launch(t + AHEAD)
        between(t, 1)
        if 0 <= t - 1 < total:
            self.stage_x(t - 1)
        between(t, 2)
        if 0 <= t - 2 < total:
            self.stage_y(t - 2)
        if 0 <= t - 3 < total:
            self.core_copy(t - 3, 1 - self.c).wait_recv()
        between(t, 3)

    def drain(self):
        units = sum(self.unit(p) * self.pieces[p][3] for p in range(len(self.pieces)))
        hidden = self.sems["ac"].shape[1]
        self.wait_bytes(self.sems["sz"].at[0], 4 * units // hidden, hidden)
        pl.when(self.middle)(lambda: self.wait_bytes(self.sems["sz"].at[1], 4 * units // hidden, hidden))
        self.wait_bytes(self.sems["sx"].at[0], 7 * units // hidden, hidden)
        self.wait_bytes(self.sems["sx"].at[1], units // hidden, hidden)
        self.wait_bytes(self.sems["sy"].at[0], 7 * units // hidden, hidden)
        for p in range(len(self.pieces)):
            if self.is_merged(p):
                self.y_one(p, 0).wait_send()
        for n in range(2):
            own = [p for p in range(len(self.pieces)) if (self.pieces[p][0] == 5) == (n == 1)]
            size = sum(self.unit(p) * self.pieces[p][3] for p in own)
            self.wait_bytes(self.sems["sk"].at[n], 24 * size // hidden, hidden)


def layer_kernel(remote, pieces, names, *refs):
    r = dict(zip(names, refs))
    tok, cot, mix, hb, acc = r["tok"], r["cot"], r["mix"], r["hb"], r["acc"]
    q, k, v, ac = r["q"], r["k"], r["v"], r["ac"]
    slopes = [r["slope%d" % n] for n in range(4)]
    fa, fb, fs = r["fa"], r["fb"], r["fs"]
    weights = [r[name] for name in ("wk", "wo", "wq", "wv", "wu", "wd")]
    wk, wo, wq, wv, wu, wd = weights
    ins = [r[name + "_in"] for name in ("wk", "wo", "wq", "wv", "wu", "wd")]
    width = tok.shape[1]
    rows = tok.shape[0]
    hidden = ac.shape[1]
    halves = [pl.ds(n * (rows // 2), rows // 2) for n in range(2)]
    chunks = [pl.ds(n * width, width) for n in range(hidden // width)]
    gain_one, shift_one, gain_two, shift_two = [
        r[name][...].reshape(1, width) for name in ("gain_one", "shift_one", "gain_two", "shift_two")
    ]
    scale_outs = [r[name][...].astype(f32).reshape(1, width) for name in ("scale_q", "scale_v")]

    def load(src, dst, n):
        return pltpu.make_async_copy(src, dst, r["load"].at[n])

    load_tok, load_cot = load(r["tok_in"], tok, 0), load(r["cot_in"], cot, 1)
    load_tok.start()
    load_cot.start()
    if remote:
        links = Links(pieces, (2, 3), ins, weights, r)
        row, rank = links.row, links.rank
        mine = pl.ds(pl.multiple_of(rank * 256, 256), 256)
        a_rows = load(r["fa_in"].at[pl.ds(pl.multiple_of(row * 96, 96), 96), :], r["a_rows"], 4)
        adapter = [
            load(r["fb_in"], fb.at[mine, :], 3),
            load(r["fa_in"], fa.at[:, mine], 2),
            load(ins[2].at[links.plane_rows(2), :], r["own_qv"].at[0], 5),
            load(ins[3].at[links.plane_rows(3), :], r["own_qv"].at[1], 6),
        ]
        a_rows.start()
        for copy in adapter:
            copy.start()
        links.greet()
        for p in range(len(pieces)):
            if not links.is_merged(p):
                links.local(p).start()
        rank_scales = [r[name][...].astype(f32).reshape(1, 256) for name in ("rank_q", "rank_v")]
        fs[:, mine] = jnp.concatenate(rank_scales + [jnp.zeros((14, 256), f32)], axis=0).astype(bf16)
        part, met = r["part"], r["met"]
        a_rows.wait()
        adapter[0].wait()
        b_rows = fb[mine, :]
        for n in range(2):
            scaled = r["a_rows"][...].astype(f32) * rank_scales[n]
            part[n] = dot(scaled.astype(bf16), b_rows).astype(bf16)
    else:
        adapter = [load(r[n + "_in"], r[n], 2 + i) for i, n in enumerate(("fa", "fb", "fs"))]
        adapter += [load(src, dst, 5 + i) for i, (src, dst) in enumerate(zip(ins, weights))]
        for copy in adapter:
            copy.start()
        for copy in adapter:
            copy.wait()

    bias, probs = [r["bias%d" % t] for t in range(4)], [r["probs%d" % t] for t in range(4)]
    segs = r["segs"][...].astype(f32)
    padded = jnp.concatenate([segs, jnp.zeros((14, segs.shape[1]), f32)], axis=0).astype(bf16)
    for b in range(2):
        pick = (lax.broadcasted_iota(jnp.int32, (16, 128), 0) == b).astype(f32).astype(bf16)
        column = dot_tn(padded, pick)
        for t, (start, size) in enumerate(WINDOWS):
            same = column[start : start + size, :] == segs[b : b + 1, 128 * t : 128 * t + 128]
            bias[t][b] = jnp.where(same, 0.0, masked_score)
    low = low_lanes()

    if remote:

        def part_rows(y, c):
            return pl.ds(pl.multiple_of(48 * c + 16 * y, 16), 32)

        places = (
            (links.y, 1 - links.c), (1 - links.y, links.c), (1 - links.y, 1 - links.c)
        )
        parts = [
            links.copy(
                part.at[:, part_rows(*place), :], met.at[n], r["sm"].at[n], r["rm"].at[n],
                links.rank_friends[n],
            )
            for n, place in enumerate(places)
        ]
        links.meet()
        for copy in parts:
            copy.start()
        for p in range(AHEAD):
            links.launch(p)
        load_tok.wait()
    else:
        load_tok.wait()

    def project(weight, out, scale):
        out[...] = (dot(tok[...], flat(weight[...])) * scale).astype(bf16)

    def attend(b, first):
        for p in range(first, first + 3):
            lanes = pl.ds(128 * p, 128)
            for t, (start, size) in enumerate(WINDOWS):
                here = pl.ds(pl.multiple_of(b * 512 + 128 * t, 128), 128)
                window = pl.ds(pl.multiple_of(b * 512 + start, 128), size)
                scores = dot_nt(k[window, lanes], two_heads(q[here, lanes], low))
                mask = bias[t][b]
                scores = jnp.where(jnp.concatenate([mask, mask], axis=1) < 0.0, masked_score, scores)
                weight = jnp.exp(scores - jnp.max(scores, axis=0, keepdims=True))
                weight = weight * (1.0 / jnp.sum(weight, axis=0, keepdims=True))
                attention = weight.astype(bf16)
                probs[t][b * (HEADS // 2) + p] = attention
                both = dot_tn(attention, v[window, lanes])
                mix[here, lanes] = jnp.where(low, both[:128], both[128:]).astype(bf16)

    def first_norm(n):
        for half in halves[n : n + 1]:
            stream = tok[half, :].astype(f32) + dot(mix[half, :], flat(wo[...]))
            normed, inverse = normalize(stream)
            r["n1"][half, :] = normed.astype(bf16)
            r["i1"][half, :] = inverse
            out = normed * gain_one + shift_one
            acc[half, :] = out
            hb[half, :] = out.astype(bf16)

    def up(n):
        proj = dot(hb[...], flat(wu[:, :, :, chunks[n]]))
        bell = jnp.exp(proj * proj * -0.5)
        area = 0.5 + 0.5 * lax.erf(proj * 0.7071067811865476)
        ac[:, chunks[n]] = (proj * area).astype(bf16)
        slopes[n][...] = (area + proj * bell * 0.3989422804014327).astype(bf16)

    third = pl.ds(0, width // 3), pl.ds(width // 3, width // 3), pl.ds(2 * (width // 3), width // 3)

    def down(n):
        acc[:, third[n]] = acc[:, third[n]] + dot(ac[...], flat(wd[:, :, :, third[n]]))

    send_out = [
        pltpu.make_async_copy(r["lo"].at[half, :], r["out"].at[half, :], r["store"].at[n])
        for n, half in enumerate(halves)
    ]

    def second_norm():
        for n, half in enumerate(halves):
            normed, inverse = normalize(acc[half, :])
            r["lo"][half, :] = (normed * gain_two + shift_two).astype(bf16)
            send_out[n].start()
            grad = norm_backward(cot[half, :].astype(f32) * gain_two, normed, inverse)
            acc[half, :] = grad
            hb[half, :] = grad.astype(bf16)

    def merge():
        for copy in adapter[1:]:
            copy.wait()
        local_units = sum(
            3 * links.unit(p) * pieces[p][3] for p in range(len(pieces)) if not links.is_merged(p)
        )
        links.wait_bytes(r["local"], local_units // width, width)
        for copy in parts:
            copy.wait_recv()
        for n, buf in enumerate((wq, wv)):
            total = part[n, part_rows(links.y, links.c), :].astype(f32)
            for slot in range(3):
                total = total + met[slot, n].astype(f32)
            joined = r["own_qv"][n].astype(f32) + total * scale_outs[n]
            buf[links.z, links.x, links.plane_rows(2 + n), :] = joined.astype(bf16)

    steps = {
        (3, 3): [lambda: project(wk, k, 1.0)],
        (5, 3): [lambda: project(wq, q, 0.125)],
        (6, 3): [lambda: project(wv, v, 1.0)],
        (7, 1): [lambda: attend(0, 0)],
        (7, 3): [lambda: attend(0, 3)],
        (8, 1): [lambda: attend(1, 0)],
        (8, 3): [lambda: attend(1, 3)],
        (9, 1): [lambda: first_norm(0)],
        (9, 2): [lambda: first_norm(1)],
        (9, 3): [lambda: up(0)],
        (10, 1): [lambda: up(1)],
        (10, 3): [lambda: up(2)],
        (11, 1): [lambda: up(3)],
        (11, 3): [lambda: down(0)],
        (12, 3): [lambda: down(1)],
        (13, 3): [lambda: down(2)],
    }
    if remote:
        steps[(0, 0)] = [merge]

    def between(t, phase):
        for step in steps.get((t, phase), ()):
            step()

    if remote:
        own_adapter = (fa.at[:, mine], fb.at[mine, :], fs.at[:, mine])
        theirs = pl.ds(pl.multiple_of(((1 - links.y) * 2 + links.c) * 256, 256), 256)
        got_adapter = (fa.at[:, theirs], fb.at[theirs, :], fs.at[:, theirs])
        core = pl.ds(pl.multiple_of((links.y * 2 + 1 - links.c) * 256, 256), 256)
        core_adapter = (fa.at[:, core], fb.at[core, :], fs.at[:, core])
        cross = pl.ds(pl.multiple_of(((1 - links.y) * 2 + 1 - links.c) * 256, 256), 256)
        cross_adapter = (fa.at[:, cross], fb.at[cross, :], fs.at[:, cross])

        def adapters(refs_, n, device):
            return [links.same(ref, r["sa"].at[n, i], r["ra"].at[n, i], device) for i, ref in enumerate(refs_)]

        for t in range(len(pieces) + 3):
            links.tick(t, between)
            if t == len(pieces) + 1:
                for copy in adapters(own_adapter, 0, links.to_y) + adapters(own_adapter, 1, links.to_core):
                    copy.start()
    else:
        for t in range(len(pieces) + 3):
            for phase in range(4):
                between(t, phase)
    load_cot.wait()
    second_norm()
    if remote:
        links.drain()
        for copy in parts:
            copy.wait_send()

    for n in range(hidden // width):
        grad = dot_nt(hb[...], wd[n].reshape(width, width))
        ac[:, chunks[n]] = (grad * slopes[n][...].astype(f32)).astype(bf16)
    for half in halves:
        grad = acc[half, :] + dot_nt(ac[half, :], flat(wu[...]))
        grad = norm_backward(grad * gain_one, r["n1"][half, :].astype(f32), r["i1"][half, :])
        acc[half, :] = grad
        hb[half, :] = grad.astype(bf16)
    grad_mix, grad_q, grad_k, grad_v = slopes
    heads = lax.broadcasted_iota(jnp.int32, (16, width), 1) // HEAD
    pick = (heads == lax.broadcasted_iota(jnp.int32, (16, width), 0)).astype(f32).astype(bf16)
    grad = dot_nt(hb[...], flat(wo[...]))
    grad_mix[...] = grad.astype(bf16)
    r["delta"][...] = dot_nt(pick, (grad * mix[...].astype(f32)).astype(bf16))
    delta = r["delta"]

    def attend_back(b, _):
        for p in range(HEADS // 2):
            lanes = pl.ds(128 * p, 128)
            keys, vals = [None] * 4, [None] * 4
            for t, (start, size) in enumerate(WINDOWS):
                here = pl.ds(pl.multiple_of(b * 512 + 128 * t, 128), 128)
                window = pl.ds(pl.multiple_of(b * 512 + start, 128), size)
                grad_pair = two_heads(grad_mix[here, lanes], low)
                grad_attn = dot_nt(v[window, lanes], grad_pair)
                attention = probs[t][b * (HEADS // 2) + p]
                centre = jnp.concatenate(
                    [delta[2 * p : 2 * p + 1, here], delta[2 * p + 1 : 2 * p + 2, here]], axis=1
                )
                grad_scores = (attention.astype(f32) * (grad_attn - centre)).astype(bf16)
                both = dot_tn(grad_scores, k[window, lanes])
                both = jnp.where(low, both[:128], both[128:]) * 0.125
                grad_q[here, lanes] = both.astype(bf16)
                key_part = dot(grad_scores, two_heads(q[here, lanes], low))
                val_part = dot(attention, grad_pair)
                for total, piece in ((keys, key_part), (vals, val_part)):
                    for n in range(size // 128):
                        at = start // 128 + n
                        add = piece[128 * n : 128 * n + 128]
                        total[at] = add if total[at] is None else total[at] + add
            for t in range(4):
                here = pl.ds(pl.multiple_of(b * 512 + 128 * t, 128), 128)
                grad_k[here, lanes] = keys[t].astype(bf16)
                grad_v[here, lanes] = vals[t].astype(bf16)
        return 0

    if remote:
        for copy in adapters(got_adapter, 0, links.to_y):
            copy.wait_recv()
        passing = adapters(got_adapter, 2, links.to_core)
        for copy in passing:
            copy.start()
    lax.fori_loop(0, 2, attend_back, 0)

    square = pl.ds(0, width)
    grads = jnp.concatenate([grad_q[...], grad_v[...]], axis=1)
    ac[square, pl.ds(0, 2 * width)] = dot_tn(tok[...], grads).astype(bf16)
    if remote:
        for refs_, n in ((core_adapter, 1), (cross_adapter, 2)):
            for copy in adapters(refs_, n, links.to_core):
                copy.wait_recv()
    for n in range(2):
        ac[:, chunks[2 + n]] = (dot_tn(fa[...], ac[square, chunks[n]]) * fb[...].astype(f32)).astype(bf16)
    out_scales = jnp.concatenate(scale_outs + [jnp.zeros((14, width), f32)], axis=0).astype(bf16)
    red = r["red"]
    red[28:32, :] = jnp.zeros((4, 128), f32)
    for n in range(2):
        along_rank = dot_nt(out_scales, ac[:, chunks[2 + n]])
        along_width = dot(fs[...], ac[:, chunks[2 + n]])
        for i in range(8):
            red[8 * n + i : 8 * n + i + 1, :] = along_rank[n : n + 1, 128 * i : 128 * i + 128]
        for i in range(6):
            at = 16 + 6 * n + i
            red[at : at + 1, :] = along_width[n : n + 1, 128 * i : 128 * i + 128]
    if remote:
        one, two = r["one"], r["two"]
        one[rank] = red[...]
        first = [
            links.copy(red, one.at[rank], r["s1"].at[n], r["r1"].at[n], friend)
            for n, friend in enumerate(links.rank_friends)
        ]
        for copy in first:
            copy.start()
    send_grad = [
        pltpu.make_async_copy(cot.at[half, :], r["grad"].at[half, :], r["store"].at[2 + n])
        for n, half in enumerate(halves)
    ]
    send_grad = [
        pltpu.make_async_copy(cot.at[half, :], r["grad"].at[half, :], r["store"].at[2 + n])
        for n, half in enumerate(halves)
    ]
    acc[...] = acc[...] + dot_nt(grad_k[...], flat(wk[...]))
    if remote:
        for copy in first:
            copy.wait_recv()
        r["sum"][...] = (one[0] + one[1]) + (one[2] + one[3])
        two[row] = r["sum"][...]
        second = [
            links.copy(r["sum"], two.at[row], r["s2"].at[n], r["r2"].at[n], friend)
            for n, friend in enumerate(links.row_friends)
        ]
        for copy in second:
            copy.start()
    for n, half in enumerate(halves):
        grad = acc[half, :] + dot_nt(grad_q[half, :], flat(wq[...]))
        grad = grad + dot_nt(grad_v[half, :], flat(wv[...]))
        cot[half, :] = grad.astype(bf16)
        send_grad[n].start()
    if remote:
        for copy in second:
            copy.wait_recv()
        total = two[0]
        for n in range(1, 8):
            total = total + two[n]
        for n, name in enumerate(("rank_grad_q", "rank_grad_v")):
            for i in range(2):
                line = jnp.zeros((1, 128), f32)
                for place in range(4):
                    at = 8 * n + 2 * place + i
                    line = jnp.where(rank == place, total[at : at + 1, :], line)
                r[name][pl.ds(128 * i, 128)] = line.reshape(128)
        for n, name in enumerate(("out_grad_q", "out_grad_v")):
            for i in range(6):
                at = 16 + 6 * n + i
                r[name][pl.ds(128 * i, 128)] = total[at : at + 1, :].reshape(128)
        for copy in first + second + passing:
            copy.wait_send()
        for copy in adapters(own_adapter, 0, links.to_y) + adapters(own_adapter, 1, links.to_core):
            copy.wait_send()
    else:
        r["small"][...] = red[...]
    for copy in send_out + send_grad:
        copy.wait()


def run_layer(remote, tokens, cotangent, weights, adapter_a, adapter_b, scales, vectors, segments):
    rows, width = tokens.shape
    hidden = weights[4].shape[-1]
    ranks = 1024
    sem = pltpu.SemaphoreType.DMA
    pieces = [(m, 96, 0, width) for m in range(4)]
    pieces += [(4, 96, n * width, width) for n in range(hidden // width)]
    pieces += [(5, 384, n * (width // 3), width // 3) for n in range(3)]
    total = len(pieces)
    block = (4, 2, width // 8, width)
    scratch = {
        "tok": pltpu.VMEM((rows, width), bf16),
        "cot": pltpu.VMEM((rows, width), bf16),
        "wk": pltpu.VMEM(block, bf16),
        "wo": pltpu.VMEM(block, bf16),
        "wq": pltpu.VMEM(block, bf16),
        "wv": pltpu.VMEM(block, bf16),
        "wu": pltpu.VMEM((4, 2, width // 8, hidden), bf16),
        "wd": pltpu.VMEM((4, 2, hidden // 8, width), bf16),
        "fa": pltpu.VMEM((width, ranks), bf16),
        "fb": pltpu.VMEM((ranks, width), bf16),
        "fs": pltpu.VMEM((16, ranks), bf16),
        "q": pltpu.VMEM((rows, width), bf16),
        "k": pltpu.VMEM((rows, width), bf16),
        "v": pltpu.VMEM((rows, width), bf16),
        "mix": pltpu.VMEM((rows, width), bf16),
        "n1": pltpu.VMEM((rows, width), bf16),
        "i1": pltpu.VMEM((rows, 1), f32),
        "hb": pltpu.VMEM((rows, width), bf16),
        "lo": pltpu.VMEM((rows, width), bf16),
        "ac": pltpu.VMEM((rows, hidden), bf16),
        "acc": pltpu.VMEM((rows, width), f32),
        "delta": pltpu.VMEM((16, rows), f32),
        "red": pltpu.VMEM((32, 128), f32),
        "load": sem((11,)),
        "store": sem((4,)),
    }
    for n in range(hidden // width):
        scratch["slope%d" % n] = pltpu.VMEM((rows, width), bf16)
    for t, (_, size) in enumerate(WINDOWS):
        scratch["bias%d" % t] = pltpu.VMEM((2, size, 128), f32)
        scratch["probs%d" % t] = pltpu.VMEM((HEADS, size, 256), bf16)
    if remote:
        scratch.update({
            "a_rows": pltpu.VMEM((96, 256), bf16),
            "own_qv": pltpu.VMEM((2, 32, width), bf16),
            "part": pltpu.VMEM((2, 96, width), bf16),
            "met": pltpu.VMEM((3, 2, 32, width), bf16),
            "one": pltpu.VMEM((4, 32, 128), f32),
            "two": pltpu.VMEM((8, 32, 128), f32),
            "sum": pltpu.VMEM((32, 128), f32),
            "local": sem(()),
            "sz": sem((2,)),
            "rz": sem((total, 3)),
            "sx": sem((2,)),
            "rw": sem((total, 2)),
            "rx": sem((total,)),
            "sy": sem((1,)),
            "ry": sem((total,)),
            "sq": sem((2,)),
            "sk": sem((2,)),
            "rk": sem((total,)),
            "sm": sem((3,)),
            "rm": sem((3,)),
            "sa": sem((3, 3)),
            "ra": sem((3, 3)),
            "s1": sem((3,)),
            "r1": sem((3,)),
            "s2": sem((7,)),
            "r2": sem((7,)),
        })
    order = ["tok_in", "cot_in", "wk_in", "wo_in", "wq_in", "wv_in", "wu_in", "wd_in", "fa_in", "fb_in"]
    given = ["gain_one", "shift_one", "gain_two", "shift_two", "scale_q", "scale_v", "segs"]
    outs = {"out": ((rows, width), bf16), "grad": ((rows, width), bf16)}
    if remote:
        given += ["rank_q", "rank_v"]
        here = ranks // 4
        outs.update({"rank_grad_q": ((here,), f32), "rank_grad_v": ((here,), f32)})
        outs.update({"out_grad_q": ((width,), f32), "out_grad_v": ((width,), f32)})
        operands = vectors + [segments] + scales
    else:
        order += ["fs_in"]
        outs["small"] = ((32, 128), f32)
        operands = scales + vectors + [segments]
    names = order + given + list(outs) + list(scratch)
    anywhere, vmem = pl.BlockSpec(memory_space=pl.ANY), pl.BlockSpec(memory_space=pltpu.VMEM)
    params = dict(vmem_limit_bytes=VMEM_LIMIT, has_side_effects=True)
    if remote:
        params["collective_id"] = 0
    return pl.pallas_call(
        partial(layer_kernel, remote, pieces, names),
        out_shape=[jax.ShapeDtypeStruct(*out) for out in outs.values()],
        in_specs=[anywhere] * len(order) + [vmem] * len(given),
        out_specs=[anywhere, anywhere] + [vmem] * (len(outs) - 2),
        scratch_shapes=list(scratch.values()),
        compiler_params=pltpu.CompilerParams(**params),
    )(tokens, cotangent, *weights, adapter_a, adapter_b, *operands)


def finish_kernel(*refs):
    ins, outs, held, loaded, stored = refs[:6], refs[6:12], refs[12:18], refs[18], refs[19]
    moves = []
    for n in range(6):
        parts = 4 if n < 2 else 1
        step = ins[n].shape[0] // parts
        for m in range(parts):
            rows, at = pl.ds(step * m, step), len(moves)
            moves.append((
                pltpu.make_async_copy(ins[n].at[rows], held[n].at[rows], loaded.at[at]),
                pltpu.make_async_copy(held[n].at[rows], outs[n].at[rows], stored.at[at]),
            ))
    for move in moves:
        move[0].start()
    for move in moves:
        move[0].wait()
        move[1].start()
    for move in moves:
        move[1].wait()


def finish(arrays):
    anywhere = pl.BlockSpec(memory_space=pl.ANY)
    return pl.pallas_call(
        finish_kernel,
        out_shape=[jax.ShapeDtypeStruct(a.shape, a.dtype) for a in arrays],
        in_specs=[anywhere] * 6,
        out_specs=[anywhere] * 6,
        scratch_shapes=[pltpu.VMEM(a.shape, a.dtype) for a in arrays]
        + [pltpu.SemaphoreType.DMA((12,))] * 2,
        compiler_params=pltpu.CompilerParams(vmem_limit_bytes=VMEM_LIMIT),
    )(*arrays)


def per_device(
    mesh_shape,
    tokens,
    w_query,
    w_key,
    w_value,
    w_out,
    w_up,
    w_down,
    gain_one,
    shift_one,
    gain_two,
    shift_two,
    adapter_a,
    adapter_b,
    query_rank_scale,
    value_rank_scale,
    query_out_scale,
    value_out_scale,
    segments,
    cotangent,
):
    vectors = [gain_one, shift_one, gain_two, shift_two, query_out_scale, value_out_scale]
    weights = [w_key, w_out, w_query, w_value, w_up, w_down]
    scales = [query_rank_scale, value_rank_scale]
    if mesh_shape == (8, 4):
        return tuple(
            finish(
                run_layer(
                    True, tokens, cotangent, weights, adapter_a, adapter_b, scales, vectors, segments
                )
            )
        )
    width = tokens.shape[1]
    rank_here = adapter_a.shape[1]
    ranks = rank_here * mesh_shape[1]
    adapter_a = lax.all_gather(adapter_a, "rank", axis=1, tiled=True)
    adapter_b = lax.all_gather(adapter_b, "rank", axis=0, tiled=True)
    scales = lax.all_gather(jnp.stack(scales), "rank", axis=1, tiled=True)
    weights = [lax.all_gather(w, "rows", axis=0, tiled=True) for w in weights]
    for n in range(2):
        added = dot(adapter_a * scales[n], adapter_b) * vectors[4 + n].astype(f32)
        weights[2 + n] = (weights[2 + n] + added).astype(bf16)
    weights = [w.reshape(4, 2, w.shape[0] // 8, w.shape[1]) for w in weights]
    scales = [jnp.pad(scales, ((0, 14), (0, 0)))]
    layer_out, input_grad, small = run_layer(
        False, tokens, cotangent, weights, adapter_a, adapter_b, scales, vectors, segments
    )
    small = lax.psum(small, ("rows", "rank")).reshape(-1)
    mine = lax.axis_index("rank") * rank_here
    return (
        layer_out,
        input_grad,
        lax.dynamic_slice(small, (mine,), (rank_here,)),
        lax.dynamic_slice(small, (ranks + mine,), (rank_here,)),
        small[2 * ranks : 2 * ranks + width],
        small[2 * ranks + width : 2 * ranks + 2 * width],
    )


def solution(mesh):
    return jax.shard_map(
        partial(per_device, (mesh.shape["rows"], mesh.shape["rank"])),
        mesh=mesh,
        in_specs=(
            P(("rows", "rank"), None),
            P("rows", None),
            P("rows", None),
            P("rows", None),
            P("rows", None),
            P("rows", None),
            P("rows", None),
            P(),
            P(),
            P(),
            P(),
            P(None, "rank"),
            P("rank", None),
            P("rank"),
            P("rank"),
            P(),
            P(),
            P(("rows", "rank"), None),
            P(("rows", "rank"), None),
        ),
        out_specs=(
            P(("rows", "rank"), None),
            P(("rows", "rank"), None),
            P("rank"),
            P("rank"),
            P(),
            P(),
        ),
        check_vma=False,
    )
```

```python
from functools import partial

import jax
import jax.numpy as jnp
from jax import lax
from jax.experimental import pallas as pl
from jax.experimental.pallas import tpu as pltpu
from jax.sharding import PartitionSpec as P

HEADS = 12
HEAD = 64
MESH = pl.DeviceIdType.MESH
epsilon = 1e-05
masked_score = -1e30
f32 = jnp.float32
bf16 = jnp.bfloat16
WINDOWS = ((0, 256), (0, 384), (128, 384), (256, 256))
AHEAD = 2
VMEM_LIMIT = 64 * 2**20


def dot(a, b):
    return jnp.dot(a, b, preferred_element_type=f32)


def dot_nt(a, b):
    return lax.dot_general(a, b, (((1,), (1,)), ((), ())), preferred_element_type=f32)


def dot_tn(a, b):
    return lax.dot_general(a, b, (((0,), (0,)), ((), ())), preferred_element_type=f32)


def flat(block):
    return block.reshape(block.shape[0] * block.shape[1] * block.shape[2], block.shape[3])


def mean(block):
    return jnp.mean(block, axis=1, keepdims=True)


def normalize(stream):
    centered = stream - mean(stream)
    inverse = lax.rsqrt(mean(centered * centered) + epsilon)
    return centered * inverse, inverse


def norm_backward(scaled, normed, inverse):
    return inverse * (scaled - mean(scaled) - normed * mean(scaled * normed))


def low_lanes():
    return lax.broadcasted_iota(jnp.int32, (128, 128), 1) < HEAD


def two_heads(block, low):
    zero = jnp.zeros_like(block)
    return jnp.concatenate([jnp.where(low, block, zero), jnp.where(low, zero, block)], axis=0)


class Links:
    def __init__(self, pieces, merged, ins, bufs, sems):
        self.pieces, self.merged, self.ins, self.bufs = pieces, merged, ins, bufs
        self.sems = sems
        self.row, self.rank = lax.axis_index("rows"), lax.axis_index("rank")
        self.z, self.x = self.row // 2, self.row % 2
        self.y, self.c = self.rank // 2, self.rank % 2
        z = self.z
        self.other = (z, z + 1 - 2 * (z % 2), (z + 2) % 4, 3 - z)
        self.middle = (z == 1) | (z == 2)
        self.to_z = [(self.other[d] * 2 + self.x, self.rank) for d in range(4)]
        self.to_x = (z * 2 + 1 - self.x, self.rank)
        self.to_y = (self.row, (1 - self.y) * 2 + self.c)
        self.to_core = (self.row, self.y * 2 + 1 - self.c)
        self.to_cross = (self.row, (1 - self.y) * 2 + 1 - self.c)
        self.rank_friends = [self.to_core, self.to_y, self.to_cross]
        self.row_friends = [
            (self.other[n // 2] * 2 + (self.x if n % 2 == 0 else 1 - self.x), self.rank)
            for n in range(1, 8)
        ]

    def greet(self):
        self.barrier = pltpu.get_barrier_semaphore()
        for friend in self.rank_friends + self.row_friends:
            pl.semaphore_signal(self.barrier, inc=1, device_id=friend, device_id_type=MESH)

    def meet(self):
        pl.semaphore_wait(self.barrier, len(self.rank_friends + self.row_friends))

    def wait_bytes(self, sem, rows, cols):
        ref = self.sems["ac"].at[pl.ds(0, rows), pl.ds(0, cols)]
        pltpu.make_async_copy(ref, ref, sem).wait()

    def copy(self, src, dst, send, recv, device):
        return pltpu.make_async_remote_copy(
            src_ref=src, dst_ref=dst, send_sem=send, recv_sem=recv,
            device_id=device, device_id_type=MESH,
        )

    def same(self, ref, send, recv, device):
        return self.copy(ref, ref, send, recv, device)

    def unit(self, p):
        return self.pieces[p][1] // 6

    def cols(self, p):
        return pl.ds(self.pieces[p][2], self.pieces[p][3])

    def plane_rows(self, p):
        u = self.unit(p)
        return pl.ds(pl.multiple_of(3 * u * self.c + u * self.y, 16), 2 * u)

    def side_rows(self, p, side):
        u = self.unit(p)
        return pl.ds(pl.multiple_of(3 * u * self.c + 2 * u * side, 16), u)

    def core_rows(self, p, core):
        u = self.unit(p)
        return pl.ds(pl.multiple_of(3 * u * core, 16), 3 * u)

    def buf(self, p):
        return self.bufs[self.pieces[p][0]]

    def is_merged(self, p):
        return self.pieces[p][0] in self.merged

    def at(self, p, z):
        return self.buf(p).at[z, self.x, self.plane_rows(p), self.cols(p)]

    def own(self, p):
        if self.is_merged(p):
            return self.at(p, self.z)
        return self.ins[self.pieces[p][0]].at[self.plane_rows(p), self.cols(p)]

    def local(self, p):
        return pltpu.make_async_copy(
            self.ins[self.pieces[p][0]].at[self.core_rows(p, self.c), self.cols(p)],
            self.buf(p).at[self.z, self.x, self.core_rows(p, self.c), self.cols(p)],
            self.sems["local"],
        )

    def z_send(self, p, d):
        return self.copy(
            self.own(p), self.at(p, self.z), self.sems["sz"].at[d // 3], self.sems["rz"].at[p, d - 1],
            self.to_z[d],
        )

    def z_pass(self, p):
        return self.same(
            self.at(p, self.other[2]), self.sems["sz"].at[1], self.sems["rz"].at[p, 2], self.to_z[1]
        )

    def z_recv(self, p, d):
        return self.same(
            self.at(p, self.other[d]), self.sems["sz"].at[0], self.sems["rz"].at[p, d - 1], self.to_z[d]
        )

    def common_rows(self, p):
        u = self.unit(p)
        return pl.ds(pl.multiple_of(3 * u * self.c + u, 16), u)

    def x_send(self, p, d):
        if d == 1:
            ref = self.buf(p).at[self.other[1], self.x, self.side_rows(p, self.y), self.cols(p)]
            return self.same(ref, self.sems["sx"].at[0], self.sems["rx"].at[p], self.to_x)
        src = self.own(p) if d == 0 else self.at(p, self.other[d])
        recv = self.sems["rw"].at[p, 0] if d == 0 else self.sems["rx"].at[p]
        return self.copy(src, self.at(p, self.other[d]), self.sems["sx"].at[0], recv, self.to_x)

    def x_own_recv(self, p):
        ref = self.buf(p).at[self.z, 1 - self.x, self.plane_rows(p), self.cols(p)]
        return self.same(ref, self.sems["sx"].at[0], self.sems["rw"].at[p, 0], self.to_x)

    def z_extra(self, p, d):
        ref = self.buf(p).at[self.other[d], 1 - self.x, self.common_rows(p), self.cols(p)]
        return self.same(ref, self.sems["sx"].at[1], self.sems["rw"].at[p, 1], self.to_z[1])

    def y_one(self, p, d):
        ref = self.buf(p).at[self.other[d], self.x, self.side_rows(p, self.y), self.cols(p)]
        send = self.sems["sy"].at[0] if d > 0 else self.sems["sq"].at[self.pieces[p][0] - 2]
        return self.same(ref, send, self.sems["ry"].at[p], self.to_y)

    def y_many(self, p):
        ref = self.buf(p).at[:, 1 - self.x, self.side_rows(p, self.y), self.cols(p)]
        return self.same(ref, self.sems["sy"].at[0], self.sems["ry"].at[p], self.to_y)

    def core_copy(self, p, core):
        ref = self.buf(p).at[:, :, self.core_rows(p, core), self.cols(p)]
        first = 0 if self.pieces[p][0] < 5 else 1
        return self.same(ref, self.sems["sk"].at[first], self.sems["rk"].at[p], self.to_core)

    def launch(self, p):
        self.z_send(p, 2).start()
        self.z_send(p, 1).start()
        pl.when(self.middle)(lambda: self.z_send(p, 3).start())
        self.x_send(p, 0).start()

    def stage_z(self, p):
        if self.is_merged(p):
            self.y_one(p, 0).start()
        for d in (2, 1, 3):
            self.z_recv(p, d).wait_recv()
            if d == 2:
                pl.when(self.middle)(lambda: self.z_pass(p).start())
            self.x_send(p, d).start()
            self.y_one(p, d).start()
        self.x_own_recv(p).wait_recv()
        self.z_extra(p, 0).start()

    def stage_x(self, p):
        self.wait_bytes(self.sems["rx"].at[p], 5 * self.unit(p), self.pieces[p][3])
        self.y_many(p).start()

    def stage_y(self, p):
        units = 8 if self.is_merged(p) else 7
        self.wait_bytes(self.sems["ry"].at[p], units * self.unit(p), self.pieces[p][3])
        self.z_extra(p, 1).wait_recv()
        self.core_copy(p, self.c).start()

    def tick(self, t, between):
        total = len(self.pieces)
        if t < total:
            self.stage_z(t)
        between(t, 0)
        if t + AHEAD < total:
            self.launch(t + AHEAD)
        between(t, 1)
        if 0 <= t - 1 < total:
            self.stage_x(t - 1)
        between(t, 2)
        if 0 <= t - 2 < total:
            self.stage_y(t - 2)
        if 0 <= t - 3 < total:
            self.core_copy(t - 3, 1 - self.c).wait_recv()
        between(t, 3)

    def drain(self):
        units = sum(self.unit(p) * self.pieces[p][3] for p in range(len(self.pieces)))
        hidden = self.sems["ac"].shape[1]
        self.wait_bytes(self.sems["sz"].at[0], 4 * units // hidden, hidden)
        pl.when(self.middle)(lambda: self.wait_bytes(self.sems["sz"].at[1], 4 * units // hidden, hidden))
        self.wait_bytes(self.sems["sx"].at[0], 7 * units // hidden, hidden)
        self.wait_bytes(self.sems["sx"].at[1], units // hidden, hidden)
        self.wait_bytes(self.sems["sy"].at[0], 7 * units // hidden, hidden)
        for p in range(len(self.pieces)):
            if self.is_merged(p):
                self.y_one(p, 0).wait_send()
        for n in range(2):
            own = [p for p in range(len(self.pieces)) if (self.pieces[p][0] == 5) == (n == 1)]
            size = sum(self.unit(p) * self.pieces[p][3] for p in own)
            self.wait_bytes(self.sems["sk"].at[n], 24 * size // hidden, hidden)


def layer_kernel(remote, pieces, names, *refs):
    r = dict(zip(names, refs))
    tok, cot, mix, hb, acc = r["tok"], r["cot"], r["mix"], r["hb"], r["acc"]
    q, k, v, ac = r["q"], r["k"], r["v"], r["ac"]
    slopes = [r["slope%d" % n] for n in range(4)]
    fa, fb, fs = r["fa"], r["fb"], r["fs"]
    weights = [r[name] for name in ("wk", "wo", "wq", "wv", "wu", "wd")]
    wk, wo, wq, wv, wu, wd = weights
    ins = [r[name + "_in"] for name in ("wk", "wo", "wq", "wv", "wu", "wd")]
    width = tok.shape[1]
    rows = tok.shape[0]
    hidden = ac.shape[1]
    halves = [pl.ds(n * (rows // 2), rows // 2) for n in range(2)]
    chunks = [pl.ds(n * width, width) for n in range(hidden // width)]
    gain_one, shift_one, gain_two, shift_two = [
        r[name][...].reshape(1, width) for name in ("gain_one", "shift_one", "gain_two", "shift_two")
    ]
    scale_outs = [r[name][...].astype(f32).reshape(1, width) for name in ("scale_q", "scale_v")]

    def load(src, dst, n):
        return pltpu.make_async_copy(src, dst, r["load"].at[n])

    load_tok, load_cot = load(r["tok_in"], tok, 0), load(r["cot_in"], cot, 1)
    if remote:
        links = Links(pieces, (2, 3), ins, weights, r)
        links.greet()
        row, rank = links.row, links.rank
        mine = pl.ds(pl.multiple_of(rank * 256, 256), 256)
        a_rows = load(r["fa_in"].at[pl.ds(pl.multiple_of(row * 96, 96), 96), :], r["a_rows"], 4)
        adapter = [
            load(r["fb_in"], fb.at[mine, :], 3),
            load(r["fa_in"], fa.at[:, mine], 2),
            load(ins[2].at[links.plane_rows(2), :], r["own_qv"].at[0], 5),
            load(ins[3].at[links.plane_rows(3), :], r["own_qv"].at[1], 6),
        ]
        a_rows.start()
        for copy in adapter:
            copy.start()
        for p in range(len(pieces)):
            if not links.is_merged(p):
                links.local(p).start()
        load_tok.start()
        load_cot.start()
        rank_scales = [r[name][...].astype(f32).reshape(1, 256) for name in ("rank_q", "rank_v")]
        fs[:, mine] = jnp.concatenate(rank_scales + [jnp.zeros((14, 256), f32)], axis=0).astype(bf16)
        part, met = r["part"], r["met"]
        a_rows.wait()
        adapter[0].wait()
        b_rows = fb[mine, :]
        for n in range(2):
            scaled = r["a_rows"][...].astype(f32) * rank_scales[n]
            part[n] = dot(scaled.astype(bf16), b_rows).astype(bf16)
    else:
        load_tok.start()
        load_cot.start()
        adapter = [load(r[n + "_in"], r[n], 2 + i) for i, n in enumerate(("fa", "fb", "fs"))]
        adapter += [load(src, dst, 5 + i) for i, (src, dst) in enumerate(zip(ins, weights))]
        for copy in adapter:
            copy.start()
        for copy in adapter:
            copy.wait()

    low = low_lanes()

    if remote:

        def part_rows(y, c):
            return pl.ds(pl.multiple_of(48 * c + 16 * y, 16), 32)

        places = (
            (links.y, 1 - links.c), (1 - links.y, links.c), (1 - links.y, 1 - links.c)
        )
        parts = [
            links.copy(
                part.at[:, part_rows(*place), :], met.at[n], r["sm"].at[n], r["rm"].at[n],
                links.rank_friends[n],
            )
            for n, place in enumerate(places)
        ]
        links.meet()
        for copy in parts:
            copy.start()
        for p in range(AHEAD):
            links.launch(p)
        load_tok.wait()
    else:
        load_tok.wait()

    bias, probs = [r["bias%d" % t] for t in range(4)], [r["probs%d" % t] for t in range(4)]
    segs = r["segs"][...].astype(f32)
    padded = jnp.concatenate([segs, jnp.zeros((14, segs.shape[1]), f32)], axis=0).astype(bf16)
    for b in range(2):
        pick = (lax.broadcasted_iota(jnp.int32, (16, 128), 0) == b).astype(f32).astype(bf16)
        column = dot_tn(padded, pick)
        for t, (start, size) in enumerate(WINDOWS):
            same = column[start : start + size, :] == segs[b : b + 1, 128 * t : 128 * t + 128]
            bias[t][b] = jnp.where(same, 0.0, masked_score)
    def project(weight, out, scale):
        out[...] = (dot(tok[...], flat(weight[...])) * scale).astype(bf16)

    def attend(b, first):
        for p in range(first, first + 3):
            lanes = pl.ds(128 * p, 128)
            for t, (start, size) in enumerate(WINDOWS):
                here = pl.ds(pl.multiple_of(b * 512 + 128 * t, 128), 128)
                window = pl.ds(pl.multiple_of(b * 512 + start, 128), size)
                scores = dot_nt(k[window, lanes], two_heads(q[here, lanes], low))
                mask = bias[t][b]
                scores = jnp.where(jnp.concatenate([mask, mask], axis=1) < 0.0, masked_score, scores)
                weight = jnp.exp(scores - jnp.max(scores, axis=0, keepdims=True))
                weight = weight * (1.0 / jnp.sum(weight, axis=0, keepdims=True))
                attention = weight.astype(bf16)
                probs[t][b * (HEADS // 2) + p] = attention
                both = dot_tn(attention, v[window, lanes])
                mix[here, lanes] = jnp.where(low, both[:128], both[128:]).astype(bf16)

    def first_norm(n):
        for half in halves[n : n + 1]:
            stream = tok[half, :].astype(f32) + dot(mix[half, :], flat(wo[...]))
            normed, inverse = normalize(stream)
            r["n1"][half, :] = normed.astype(bf16)
            r["i1"][half, :] = inverse
            out = normed * gain_one + shift_one
            acc[half, :] = out
            hb[half, :] = out.astype(bf16)

    def up(n):
        proj = dot(hb[...], flat(wu[:, :, :, chunks[n]]))
        bell = jnp.exp(proj * proj * -0.5)
        area = 0.5 + 0.5 * lax.erf(proj * 0.7071067811865476)
        ac[:, chunks[n]] = (proj * area).astype(bf16)
        slopes[n][...] = (area + proj * bell * 0.3989422804014327).astype(bf16)

    third = pl.ds(0, width // 3), pl.ds(width // 3, width // 3), pl.ds(2 * (width // 3), width // 3)

    def down(n):
        acc[:, third[n]] = acc[:, third[n]] + dot(ac[...], flat(wd[:, :, :, third[n]]))

    send_out = [
        pltpu.make_async_copy(r["lo"].at[half, :], r["out"].at[half, :], r["store"].at[n])
        for n, half in enumerate(halves)
    ]

    def second_norm():
        for n, half in enumerate(halves):
            normed, inverse = normalize(acc[half, :])
            r["lo"][half, :] = (normed * gain_two + shift_two).astype(bf16)
            send_out[n].start()
            grad = norm_backward(cot[half, :].astype(f32) * gain_two, normed, inverse)
            acc[half, :] = grad
            hb[half, :] = grad.astype(bf16)

    def merge():
        for copy in adapter[1:]:
            copy.wait()
        local_units = sum(
            3 * links.unit(p) * pieces[p][3] for p in range(len(pieces)) if not links.is_merged(p)
        )
        links.wait_bytes(r["local"], local_units // width, width)
        for copy in parts:
            copy.wait_recv()
        for n, buf in enumerate((wq, wv)):
            total = part[n, part_rows(links.y, links.c), :].astype(f32)
            for slot in range(3):
                total = total + met[slot, n].astype(f32)
            joined = r["own_qv"][n].astype(f32) + total * scale_outs[n]
            buf[links.z, links.x, links.plane_rows(2 + n), :] = joined.astype(bf16)

    steps = {
        (3, 3): [lambda: project(wk, k, 1.0)],
        (5, 3): [lambda: project(wq, q, 0.125)],
        (6, 3): [lambda: project(wv, v, 1.0)],
        (7, 1): [lambda: attend(0, 0)],
        (7, 3): [lambda: attend(0, 3)],
        (8, 1): [lambda: attend(1, 0)],
        (8, 3): [lambda: attend(1, 3)],
        (9, 1): [lambda: first_norm(0)],
        (9, 2): [lambda: first_norm(1)],
        (9, 3): [lambda: up(0)],
        (10, 1): [lambda: up(1)],
        (10, 3): [lambda: up(2)],
        (11, 1): [lambda: up(3)],
        (11, 3): [lambda: down(0)],
        (12, 3): [lambda: down(1)],
        (13, 3): [lambda: down(2)],
    }
    if remote:
        steps[(0, 0)] = [merge]

    def between(t, phase):
        for step in steps.get((t, phase), ()):
            step()

    if remote:
        own_adapter = (fa.at[:, mine], fb.at[mine, :], fs.at[:, mine])
        theirs = pl.ds(pl.multiple_of(((1 - links.y) * 2 + links.c) * 256, 256), 256)
        got_adapter = (fa.at[:, theirs], fb.at[theirs, :], fs.at[:, theirs])
        core = pl.ds(pl.multiple_of((links.y * 2 + 1 - links.c) * 256, 256), 256)
        core_adapter = (fa.at[:, core], fb.at[core, :], fs.at[:, core])
        cross = pl.ds(pl.multiple_of(((1 - links.y) * 2 + 1 - links.c) * 256, 256), 256)
        cross_adapter = (fa.at[:, cross], fb.at[cross, :], fs.at[:, cross])

        def adapters(refs_, n, device):
            return [links.same(ref, r["sa"].at[n, i], r["ra"].at[n, i], device) for i, ref in enumerate(refs_)]

        for t in range(len(pieces) + 3):
            links.tick(t, between)
            if t == len(pieces) + 1:
                for copy in adapters(own_adapter, 0, links.to_y) + adapters(own_adapter, 1, links.to_core):
                    copy.start()
    else:
        for t in range(len(pieces) + 3):
            for phase in range(4):
                between(t, phase)
    load_cot.wait()
    second_norm()
    if remote:
        links.drain()
        for copy in parts:
            copy.wait_send()

    for n in range(hidden // width):
        grad = dot_nt(hb[...], wd[n].reshape(width, width))
        ac[:, chunks[n]] = (grad * slopes[n][...].astype(f32)).astype(bf16)
    for half in halves:
        grad = acc[half, :] + dot_nt(ac[half, :], flat(wu[...]))
        grad = norm_backward(grad * gain_one, r["n1"][half, :].astype(f32), r["i1"][half, :])
        acc[half, :] = grad
        hb[half, :] = grad.astype(bf16)
    grad_mix, grad_q, grad_k, grad_v = slopes
    heads = lax.broadcasted_iota(jnp.int32, (16, width), 1) // HEAD
    pick = (heads == lax.broadcasted_iota(jnp.int32, (16, width), 0)).astype(f32).astype(bf16)
    grad = dot_nt(hb[...], flat(wo[...]))
    grad_mix[...] = grad.astype(bf16)
    r["delta"][...] = dot_nt(pick, (grad * mix[...].astype(f32)).astype(bf16))
    delta = r["delta"]

    def attend_back(b, _):
        for p in range(HEADS // 2):
            lanes = pl.ds(128 * p, 128)
            keys, vals = [None] * 4, [None] * 4
            for t, (start, size) in enumerate(WINDOWS):
                here = pl.ds(pl.multiple_of(b * 512 + 128 * t, 128), 128)
                window = pl.ds(pl.multiple_of(b * 512 + start, 128), size)
                grad_pair = two_heads(grad_mix[here, lanes], low)
                grad_attn = dot_nt(v[window, lanes], grad_pair)
                attention = probs[t][b * (HEADS // 2) + p]
                centre = jnp.concatenate(
                    [delta[2 * p : 2 * p + 1, here], delta[2 * p + 1 : 2 * p + 2, here]], axis=1
                )
                grad_scores = (attention.astype(f32) * (grad_attn - centre)).astype(bf16)
                both = dot_tn(grad_scores, k[window, lanes])
                both = jnp.where(low, both[:128], both[128:]) * 0.125
                grad_q[here, lanes] = both.astype(bf16)
                key_part = dot(grad_scores, two_heads(q[here, lanes], low))
                val_part = dot(attention, grad_pair)
                for total, piece in ((keys, key_part), (vals, val_part)):
                    for n in range(size // 128):
                        at = start // 128 + n
                        add = piece[128 * n : 128 * n + 128]
                        total[at] = add if total[at] is None else total[at] + add
            for t in range(4):
                here = pl.ds(pl.multiple_of(b * 512 + 128 * t, 128), 128)
                grad_k[here, lanes] = keys[t].astype(bf16)
                grad_v[here, lanes] = vals[t].astype(bf16)
        return 0

    if remote:
        for copy in adapters(got_adapter, 0, links.to_y):
            copy.wait_recv()
        passing = adapters(got_adapter, 2, links.to_core)
        for copy in passing:
            copy.start()
    lax.fori_loop(0, 2, attend_back, 0)

    square = pl.ds(0, width)
    grads = jnp.concatenate([grad_q[...], grad_v[...]], axis=1)
    ac[square, pl.ds(0, 2 * width)] = dot_tn(tok[...], grads).astype(bf16)
    if remote:
        for refs_, n in ((core_adapter, 1), (cross_adapter, 2)):
            for copy in adapters(refs_, n, links.to_core):
                copy.wait_recv()
    for n in range(2):
        ac[:, chunks[2 + n]] = (dot_tn(fa[...], ac[square, chunks[n]]) * fb[...].astype(f32)).astype(bf16)
    out_scales = jnp.concatenate(scale_outs + [jnp.zeros((14, width), f32)], axis=0).astype(bf16)
    red = r["red"]
    red[28:32, :] = jnp.zeros((4, 128), f32)
    for n in range(2):
        along_rank = dot_nt(out_scales, ac[:, chunks[2 + n]])
        along_width = dot(fs[...], ac[:, chunks[2 + n]])
        for i in range(8):
            red[8 * n + i : 8 * n + i + 1, :] = along_rank[n : n + 1, 128 * i : 128 * i + 128]
        for i in range(6):
            at = 16 + 6 * n + i
            red[at : at + 1, :] = along_width[n : n + 1, 128 * i : 128 * i + 128]
    if remote:
        one, two = r["one"], r["two"]
        one[rank] = red[...]
        first = [
            links.copy(red, one.at[rank], r["s1"].at[n], r["r1"].at[n], friend)
            for n, friend in enumerate(links.rank_friends)
        ]
        for copy in first:
            copy.start()
    send_grad = [
        pltpu.make_async_copy(cot.at[half, :], r["grad"].at[half, :], r["store"].at[2 + n])
        for n, half in enumerate(halves)
    ]
    send_grad = [
        pltpu.make_async_copy(cot.at[half, :], r["grad"].at[half, :], r["store"].at[2 + n])
        for n, half in enumerate(halves)
    ]
    acc[...] = acc[...] + dot_nt(grad_k[...], flat(wk[...]))
    acc[halves[0], :] = acc[halves[0], :] + dot_nt(grad_q[halves[0], :], flat(wq[...]))
    if remote:
        for copy in first:
            copy.wait_recv()
        r["sum"][...] = (one[0] + one[1]) + (one[2] + one[3])
        two[row] = r["sum"][...]
        second = [
            links.copy(r["sum"], two.at[row], r["s2"].at[n], r["r2"].at[n], friend)
            for n, friend in enumerate(links.row_friends)
        ]
        for copy in second:
            copy.start()
    for n, half in enumerate(halves):
        grad = acc[half, :] + dot_nt(grad_v[half, :], flat(wv[...]))
        if n == 1:
            grad = grad + dot_nt(grad_q[half, :], flat(wq[...]))
        cot[half, :] = grad.astype(bf16)
        send_grad[n].start()
    if remote:
        for copy in second:
            copy.wait_recv()
        total = two[0]
        for n in range(1, 8):
            total = total + two[n]
        for n, name in enumerate(("rank_grad_q", "rank_grad_v")):
            for i in range(2):
                line = jnp.zeros((1, 128), f32)
                for place in range(4):
                    at = 8 * n + 2 * place + i
                    line = jnp.where(rank == place, total[at : at + 1, :], line)
                r[name][pl.ds(128 * i, 128)] = line.reshape(128)
        for n, name in enumerate(("out_grad_q", "out_grad_v")):
            for i in range(6):
                at = 16 + 6 * n + i
                r[name][pl.ds(128 * i, 128)] = total[at : at + 1, :].reshape(128)
        for copy in first + second + passing:
            copy.wait_send()
        for copy in adapters(own_adapter, 0, links.to_y) + adapters(own_adapter, 1, links.to_core):
            copy.wait_send()
    else:
        r["small"][...] = red[...]
    for copy in send_out + send_grad:
        copy.wait()


def run_layer(remote, tokens, cotangent, weights, adapter_a, adapter_b, scales, vectors, segments):
    rows, width = tokens.shape
    hidden = weights[4].shape[-1]
    ranks = 1024
    sem = pltpu.SemaphoreType.DMA
    pieces = [(m, 96, 0, width) for m in range(4)]
    pieces += [(4, 96, n * width, width) for n in range(hidden // width)]
    pieces += [(5, 384, n * (width // 3), width // 3) for n in range(3)]
    total = len(pieces)
    block = (4, 2, width // 8, width)
    scratch = {
        "tok": pltpu.VMEM((rows, width), bf16),
        "cot": pltpu.VMEM((rows, width), bf16),
        "wk": pltpu.VMEM(block, bf16),
        "wo": pltpu.VMEM(block, bf16),
        "wq": pltpu.VMEM(block, bf16),
        "wv": pltpu.VMEM(block, bf16),
        "wu": pltpu.VMEM((4, 2, width // 8, hidden), bf16),
        "wd": pltpu.VMEM((4, 2, hidden // 8, width), bf16),
        "fa": pltpu.VMEM((width, ranks), bf16),
        "fb": pltpu.VMEM((ranks, width), bf16),
        "fs": pltpu.VMEM((16, ranks), bf16),
        "q": pltpu.VMEM((rows, width), bf16),
        "k": pltpu.VMEM((rows, width), bf16),
        "v": pltpu.VMEM((rows, width), bf16),
        "mix": pltpu.VMEM((rows, width), bf16),
        "n1": pltpu.VMEM((rows, width), bf16),
        "i1": pltpu.VMEM((rows, 1), f32),
        "hb": pltpu.VMEM((rows, width), bf16),
        "lo": pltpu.VMEM((rows, width), bf16),
        "ac": pltpu.VMEM((rows, hidden), bf16),
        "acc": pltpu.VMEM((rows, width), f32),
        "delta": pltpu.VMEM((16, rows), f32),
        "red": pltpu.VMEM((32, 128), f32),
        "load": sem((11,)),
        "store": sem((4,)),
    }
    for n in range(hidden // width):
        scratch["slope%d" % n] = pltpu.VMEM((rows, width), bf16)
    for t, (_, size) in enumerate(WINDOWS):
        scratch["bias%d" % t] = pltpu.VMEM((2, size, 128), f32)
        scratch["probs%d" % t] = pltpu.VMEM((HEADS, size, 256), bf16)
    if remote:
        scratch.update({
            "a_rows": pltpu.VMEM((96, 256), bf16),
            "own_qv": pltpu.VMEM((2, 32, width), bf16),
            "part": pltpu.VMEM((2, 96, width), bf16),
            "met": pltpu.VMEM((3, 2, 32, width), bf16),
            "one": pltpu.VMEM((4, 32, 128), f32),
            "two": pltpu.VMEM((8, 32, 128), f32),
            "sum": pltpu.VMEM((32, 128), f32),
            "local": sem(()),
            "sz": sem((2,)),
            "rz": sem((total, 3)),
            "sx": sem((2,)),
            "rw": sem((total, 2)),
            "rx": sem((total,)),
            "sy": sem((1,)),
            "ry": sem((total,)),
            "sq": sem((2,)),
            "sk": sem((2,)),
            "rk": sem((total,)),
            "sm": sem((3,)),
            "rm": sem((3,)),
            "sa": sem((3, 3)),
            "ra": sem((3, 3)),
            "s1": sem((3,)),
            "r1": sem((3,)),
            "s2": sem((7,)),
            "r2": sem((7,)),
        })
    order = ["tok_in", "cot_in", "wk_in", "wo_in", "wq_in", "wv_in", "wu_in", "wd_in", "fa_in", "fb_in"]
    given = ["gain_one", "shift_one", "gain_two", "shift_two", "scale_q", "scale_v", "segs"]
    outs = {"out": ((rows, width), bf16), "grad": ((rows, width), bf16)}
    if remote:
        given += ["rank_q", "rank_v"]
        here = ranks // 4
        outs.update({"rank_grad_q": ((here,), f32), "rank_grad_v": ((here,), f32)})
        outs.update({"out_grad_q": ((width,), f32), "out_grad_v": ((width,), f32)})
        operands = vectors + [segments] + scales
    else:
        order += ["fs_in"]
        outs["small"] = ((32, 128), f32)
        operands = scales + vectors + [segments]
    names = order + given + list(outs) + list(scratch)
    anywhere, vmem = pl.BlockSpec(memory_space=pl.ANY), pl.BlockSpec(memory_space=pltpu.VMEM)
    params = dict(vmem_limit_bytes=VMEM_LIMIT, has_side_effects=True)
    if remote:
        params["collective_id"] = 0
    return pl.pallas_call(
        partial(layer_kernel, remote, pieces, names),
        out_shape=[jax.ShapeDtypeStruct(*out) for out in outs.values()],
        in_specs=[anywhere] * len(order) + [vmem] * len(given),
        out_specs=[anywhere, anywhere] + [vmem] * (len(outs) - 2),
        scratch_shapes=list(scratch.values()),
        compiler_params=pltpu.CompilerParams(**params),
    )(tokens, cotangent, *weights, adapter_a, adapter_b, *operands)


def finish_kernel(*refs):
    ins, outs, held, loaded, stored = refs[:6], refs[6:12], refs[12:18], refs[18], refs[19]
    moves = []
    for n in range(6):
        parts = 4 if n < 2 else 1
        step = ins[n].shape[0] // parts
        for m in range(parts):
            rows, at = pl.ds(step * m, step), len(moves)
            moves.append((
                pltpu.make_async_copy(ins[n].at[rows], held[n].at[rows], loaded.at[at]),
                pltpu.make_async_copy(held[n].at[rows], outs[n].at[rows], stored.at[at]),
            ))
    for move in moves:
        move[0].start()
    for move in moves:
        move[0].wait()
        move[1].start()
    for move in moves:
        move[1].wait()


def finish(arrays):
    anywhere = pl.BlockSpec(memory_space=pl.ANY)
    return pl.pallas_call(
        finish_kernel,
        out_shape=[jax.ShapeDtypeStruct(a.shape, a.dtype) for a in arrays],
        in_specs=[anywhere] * 6,
        out_specs=[anywhere] * 6,
        scratch_shapes=[pltpu.VMEM(a.shape, a.dtype) for a in arrays]
        + [pltpu.SemaphoreType.DMA((12,))] * 2,
        compiler_params=pltpu.CompilerParams(vmem_limit_bytes=VMEM_LIMIT),
    )(*arrays)


def per_device(
    mesh_shape,
    tokens,
    w_query,
    w_key,
    w_value,
    w_out,
    w_up,
    w_down,
    gain_one,
    shift_one,
    gain_two,
    shift_two,
    adapter_a,
    adapter_b,
    query_rank_scale,
    value_rank_scale,
    query_out_scale,
    value_out_scale,
    segments,
    cotangent,
):
    vectors = [gain_one, shift_one, gain_two, shift_two, query_out_scale, value_out_scale]
    weights = [w_key, w_out, w_query, w_value, w_up, w_down]
    scales = [query_rank_scale, value_rank_scale]
    if mesh_shape == (8, 4):
        return tuple(
            finish(
                run_layer(
                    True, tokens, cotangent, weights, adapter_a, adapter_b, scales, vectors, segments
                )
            )
        )
    width = tokens.shape[1]
    rank_here = adapter_a.shape[1]
    ranks = rank_here * mesh_shape[1]
    adapter_a = lax.all_gather(adapter_a, "rank", axis=1, tiled=True)
    adapter_b = lax.all_gather(adapter_b, "rank", axis=0, tiled=True)
    scales = lax.all_gather(jnp.stack(scales), "rank", axis=1, tiled=True)
    weights = [lax.all_gather(w, "rows", axis=0, tiled=True) for w in weights]
    for n in range(2):
        added = dot(adapter_a * scales[n], adapter_b) * vectors[4 + n].astype(f32)
        weights[2 + n] = (weights[2 + n] + added).astype(bf16)
    weights = [w.reshape(4, 2, w.shape[0] // 8, w.shape[1]) for w in weights]
    scales = [jnp.pad(scales, ((0, 14), (0, 0)))]
    layer_out, input_grad, small = run_layer(
        False, tokens, cotangent, weights, adapter_a, adapter_b, scales, vectors, segments
    )
    small = lax.psum(small, ("rows", "rank")).reshape(-1)
    mine = lax.axis_index("rank") * rank_here
    return (
        layer_out,
        input_grad,
        lax.dynamic_slice(small, (mine,), (rank_here,)),
        lax.dynamic_slice(small, (ranks + mine,), (rank_here,)),
        small[2 * ranks : 2 * ranks + width],
        small[2 * ranks + width : 2 * ranks + 2 * width],
    )


def solution(mesh):
    return jax.shard_map(
        partial(per_device, (mesh.shape["rows"], mesh.shape["rank"])),
        mesh=mesh,
        in_specs=(
            P(("rows", "rank"), None),
            P("rows", None),
            P("rows", None),
            P("rows", None),
            P("rows", None),
            P("rows", None),
            P("rows", None),
            P(),
            P(),
            P(),
            P(),
            P(None, "rank"),
            P("rank", None),
            P("rank"),
            P("rank"),
            P(),
            P(),
            P(("rows", "rank"), None),
            P(("rows", "rank"), None),
        ),
        out_specs=(
            P(("rows", "rank"), None),
            P(("rows", "rank"), None),
            P("rank"),
            P("rank"),
            P(),
            P(),
        ),
        check_vma=False,
    )
```
